512 devices in a mesh: clip: 64 (over x, z), dp: 8 (over y, core).
Axes of the slice: x: 4, y: 4, z: 16, core: 2. Of those that a mesh axis runs over, the one named last changes fastest.
Arguments:
- video_latents: bfloat16 [8, 2, 64, 4, 8, 768], P('dp', None, 'clip'), may hold values from -6 to 6
- cotangent: bfloat16 [8, 2, 64, 4, 8, 768], P('dp', None, 'clip'), may hold values from -6 to 6
- conv_weight: bfloat16 [3, 3, 3, 96, 384], P(None, None, None, 'dp'), may hold values from -0.078125 to 0.078125
- norm_gain: float32 [192], replicated, may hold values from 0.1 to 1.9
- clip_lengths: int32 [8, 12], P('dp'), may hold values from 1 to 20, 128 in all within a row
Outputs:
- decoded: bfloat16 [8, 2, 64, 4, 8, 768], P('dp', None, 'clip')
- latent_grad: bfloat16 [8, 2, 64, 4, 8, 768], P('dp', None, 'clip')
- weight_grad: float32 [3, 3, 3, 96, 384], P(None, None, None, 'dp')
- gain_grad: float32 [192], replicated
The draws below stay inside these ranges and needn't reach their ends.
Inputs may be any that keep to these rules, and one draw needn't show every extreme that they name: `clip_lengths`: each replica's lengths sum to 128; in every replica some clip is exactly 20 groups long.
All inputs are finite; a program needn't handle non-finite values.
Results may differ from the reference program's by a relative error of at most 0.01.
Values may be sent and summed in bfloat16 or wider, within the bound.
No kernel may reach another device: no remote copies, remote signals or barrier semaphores. Data moves between devices by JAX's collectives and lax.ppermute only.
A program may use at most 128 MiB of HBM per device.

```python
import math
import jax
import jax.numpy as jnp
import numpy as np
from jax import lax

C = 192
FRAMES = 4
TILE_H = 8
TILE_W = 4
WAVES = 2
MOST = 20
LANES = 64
REPLICAS = 8
GROUPS = 128
NCLIPS = 12


def steps_of(key, extent, shards, smallest, top_value):
    level = 1.0
    for axis_at, blocks in shards:
        draws = jax.random.uniform(jax.random.fold_in(jax.random.fold_in(key, 6), axis_at), (blocks,), jnp.float32, smallest / len(shards), top_value / len(shards))
        level = level * jnp.repeat(jnp.exp(draws), extent[axis_at] // blocks).reshape((-1,) + (1,) * (len(extent) - 1 - axis_at))
    return level


def split_up(count, total, reach, skew):
    loads = [(1 << 20) // math.isqrt(standing ** skew) + 1 for standing in range(2, count + 1)]
    spare, given = total - reach - (count - 1), [1] * (count - 1)
    while spare > 0:
        candidates = [i for i in range(count - 1) if given[i] < reach]
        whole, left = sum([loads[i] for i in candidates]), spare
        for i in candidates:
            addition = min(reach - given[i], max(1, left * loads[i] // whole), spare)
            given[i] = given[i] + addition
            spare = spare - addition
    return np.array([reach] + given)


def uneven_parts(rng, amount, total, bound, lean):
    if amount == 2:
        one = jax.random.randint(rng, (), max(1, total - bound), min(bound, total - 1) + 1)
        return jnp.stack([one, total - one])
    sizes = jnp.asarray(split_up(amount, total, bound, lean), jnp.int32)
    twos = (amount - 1) // 2
    donor, sink = sizes[1:1 + 2 * twos:2], sizes[2:2 + 2 * twos:2]
    room = jnp.minimum(donor - 1, bound - sink)
    passed = jax.random.randint(jax.random.fold_in(rng, 1), (twos,), 0, 1 << 20) % (room + 1)
    sizes = sizes.at[1:1 + 2 * twos:2].set(donor - passed).at[2:2 + 2 * twos:2].set(sink + passed)
    return sizes[jax.random.permutation(jax.random.fold_in(rng, 2), amount)]


def gaussian(rng, dims, spread, limit, split=(), held_as=jnp.bfloat16):
    entries = spread * jax.random.normal(rng, dims, jnp.float32)
    if split:
        entries = entries * steps_of(rng, dims, split, -0.22, 0.18)
    return jnp.clip(entries, -limit, limit).astype(held_as)


def setup_inputs(seed: int = 0) -> dict:
    streams_of = jax.random.split(jax.random.key(seed), 6)
    video_latents = gaussian(streams_of[0], (REPLICAS, WAVES, LANES, FRAMES, TILE_H, TILE_W * C), 1.0, 6.0, ((0, 8), (2, 64)))
    cotangent = gaussian(streams_of[1], (REPLICAS, WAVES, LANES, FRAMES, TILE_H, TILE_W * C), 1.0, 6.0, ((0, 8), (2, 64)))
    conv_weight = gaussian(streams_of[2], (3, 3, 3, C // 2, 2 * C), (27 * C) ** -0.5, 0.078125, ((3, 8),))
    norm_gain = jnp.clip(1.0 + 0.18 * jax.random.normal(streams_of[3], (C,), jnp.float32), 0.1, 1.9)
    clip_lengths = jax.vmap(lambda own: uneven_parts(own, NCLIPS, GROUPS, MOST, 2))(jax.random.split(streams_of[4], REPLICAS)).reshape((REPLICAS, NCLIPS)).astype(jnp.int32)
    return {"video_latents": video_latents, "cotangent": cotangent, "conv_weight": conv_weight, "norm_gain": norm_gain, "clip_lengths": clip_lengths}


epsilon = 1e-06

def clip_info(lengths, order):
    ends = jnp.cumsum(lengths)
    begins = ends - lengths
    starting = jnp.any(begins[None, :] == order[:, None], axis=1)
    member = (order[:, None] >= begins[None, :]) & (order[:, None] < ends[None, :])
    inverse = 1.0 / lengths.astype(jnp.float32)
    group_weight = lax.optimization_barrier(jnp.sum(jnp.where(member, inverse[None, :], jnp.float32(0.0)), axis=1))
    return (jnp.logical_not(starting), group_weight)

def activate(latent, norm_gain):
    values = latent.astype(jnp.float32)
    scale = lax.rsqrt(lax.optimization_barrier(jnp.mean(values * values, axis=-1, keepdims=True)) + epsilon)
    normed = values * scale
    act = normed * norm_gain
    hidden = (act * jax.nn.sigmoid(act)).astype(jnp.bfloat16)
    return (hidden, normed, scale, act)

def activate_back(hidden_grad, normed, scale, act, norm_gain):
    sigma = jax.nn.sigmoid(act)
    act_grad = hidden_grad * sigma * (1.0 + act * (1.0 - sigma))
    gain_part = lax.optimization_barrier(jnp.sum((act_grad * normed).reshape(-1, act.shape[-1]), axis=0))
    inner = act_grad * norm_gain
    latent_part = scale * (inner - normed * lax.optimization_barrier(jnp.mean(inner * normed, axis=-1, keepdims=True)))
    return (latent_part, gain_part)

def shifted(padded, depth, height, frames, rows, columns):
    return jnp.concatenate([padded[:, depth:depth + frames, height:height + rows, width:width + columns, :] for width in range(3)], axis=-1)

def conv_forward(padded, kernel):
    batch, frames, rows, columns = (padded.shape[0], padded.shape[1] - 2, padded.shape[2] - 2, padded.shape[3] - 2)
    inputs_count, outputs_count = (kernel.shape[3], kernel.shape[4])
    total = jnp.zeros((batch * frames * rows * columns, outputs_count), jnp.float32)
    for depth in range(3):
        for height in range(3):
            block = shifted(padded, depth, height, frames, rows, columns).reshape(-1, 3 * inputs_count)
            total = total + jnp.dot(block, kernel[depth, height].reshape(3 * inputs_count, outputs_count), preferred_element_type=jnp.float32)
    return total.reshape(batch, frames, rows, columns, outputs_count)

def conv_adjoint(upstream, kernel):
    batch, frames, rows, columns, outputs_count = upstream.shape
    inputs_count = kernel.shape[3]
    wide = jnp.pad(upstream, ((0, 0), (2, 2), (2, 2), (2, 2), (0, 0)))
    total = jnp.zeros((batch * (frames + 2) * (rows + 2) * (columns + 2), inputs_count), jnp.float32)
    for depth in range(3):
        for height in range(3):
            block = jnp.concatenate([wide[:, 2 - depth:4 - depth + frames, 2 - height:4 - height + rows, 2 - width:4 - width + columns, :] for width in range(3)], axis=-1)
            matrix = jnp.transpose(kernel[depth, height], (0, 2, 1)).reshape(3 * outputs_count, inputs_count)
            total = total + jnp.dot(block.reshape(-1, 3 * outputs_count), matrix, preferred_element_type=jnp.float32)
    return total.reshape(batch, frames + 2, rows + 2, columns + 2, inputs_count)

def kernel_grad(padded, upstream):
    batch, frames, rows, columns, outputs_count = upstream.shape
    inputs_count = padded.shape[4]
    flat = upstream.reshape(-1, outputs_count)
    layers = []
    for depth in range(3):
        row_list = []
        for height in range(3):
            block = shifted(padded, depth, height, frames, rows, columns).reshape(-1, 3 * inputs_count)
            part = lax.dot_general(block, flat, (((0,), (0,)), ((), ())), preferred_element_type=jnp.float32)
            row_list.append(part.reshape(3, inputs_count, outputs_count))
        layers.append(jnp.stack(row_list, axis=0))
    return jnp.stack(layers, axis=0)

def pad_space(frames_array):
    return jnp.pad(frames_array, ((0, 0), (0, 0), (1, 1), (1, 1), (0, 0)))

def one_replica(latents, cotangent, lengths, kernel, norm_gain):
    channels = norm_gain.shape[0]
    merged_shape = latents.shape
    groups = merged_shape[0] * merged_shape[1]
    frames, rows = (merged_shape[2], merged_shape[3])
    columns = merged_shape[4] // channels
    cell_shape = (groups, frames, rows, columns, channels)
    latent = latents.reshape(cell_shape)
    upstream_raw = cotangent.reshape(cell_shape)
    order = jnp.arange(groups, dtype=jnp.int32)
    same, group_weight = clip_info(lengths, order)
    hidden, normed, scale, act = activate(latent, norm_gain)
    earlier = jnp.concatenate([jnp.zeros_like(hidden[:1, frames - 2:]), hidden[:-1, frames - 2:]], axis=0)
    earlier = jnp.where(same[:, None, None, None, None], earlier, jnp.zeros_like(earlier))
    padded = pad_space(jnp.concatenate([earlier, hidden], axis=1))
    decoded = (latent.astype(jnp.float32) + conv_forward(padded, kernel)).astype(jnp.bfloat16)
    upstream = (upstream_raw.astype(jnp.float32) * group_weight[:, None, None, None, None]).astype(jnp.bfloat16)
    weight_part = kernel_grad(padded, upstream)
    padded_grad = conv_adjoint(upstream, kernel)[:, :, 1:-1, 1:-1]
    cache_grad = jnp.where(same[:, None, None, None, None], padded_grad[:, :2], jnp.float32(0.0))
    carried = jnp.concatenate([cache_grad[1:], jnp.zeros_like(cache_grad[:1])], axis=0)
    hidden_grad = padded_grad[:, 2:] + jnp.pad(carried, ((0, 0), (frames - 2, 0), (0, 0), (0, 0), (0, 0)))
    latent_part, gain_part = activate_back(hidden_grad, normed, scale, act, norm_gain)
    latent_grad = (upstream.astype(jnp.float32) + latent_part).astype(jnp.bfloat16)
    return (decoded.reshape(merged_shape), latent_grad.reshape(merged_shape), weight_part, gain_part)

def reference(video_latents, cotangent, conv_weight, norm_gain, clip_lengths):
    channels = norm_gain.shape[0]
    kernel = conv_weight.reshape(3, 3, 3, channels, channels)

    def step(items):
        return one_replica(items[0], items[1], items[2], kernel, norm_gain)
    decoded, latent_grad, weight_parts, gain_parts = lax.map(step, (video_latents, cotangent, clip_lengths))
    weight_total = lax.optimization_barrier(jnp.sum(weight_parts, axis=0)).reshape(conv_weight.shape)
    return (decoded, latent_grad, weight_total, lax.optimization_barrier(jnp.sum(gain_parts, axis=0)))
```

```python
import functools

import jax
import jax.numpy as jnp
from jax import lax
from jax.experimental import pallas as pl
from jax.experimental.pallas import tpu as pltpu
from jax.sharding import Mesh, PartitionSpec as P

epsilon = 1e-06
bf16 = jnp.bfloat16
f32 = jnp.float32
C = 192
NX, NH, NL, NY, NCORE = 4, 4, 4, 4, 2
LANES = NX * NH * NL
VMEM_LIMIT = 24 * 1024 * 1024


def scalars(numbers_ref):
    count = numbers_ref.shape[0] - 2
    lane = numbers_ref[count]
    infos = []
    for wave in range(2):
        q = wave * LANES + lane
        begin = jnp.int32(0)
        length = jnp.int32(0)
        starts = jnp.int32(0)
        next_starts = jnp.int32(0)
        for k in range(count):
            own = numbers_ref[k]
            end = begin + own
            inside = jnp.logical_and(q >= begin, q < end)
            length = length + jnp.where(inside, own, 0)
            starts = starts + jnp.where(q == begin, 1, 0)
            next_starts = next_starts + jnp.where(q + 1 == begin, 1, 0)
            begin = end
        same = jnp.where(starts == 0, 1, 0)
        following = jnp.where(
            jnp.logical_and(next_starts == 0, q + 1 < 2 * LANES), 1, 0
        )
        infos.append((length, same, following))
    return lane, numbers_ref[count + 1], infos


def per_row(first, second):
    row = lax.broadcasted_iota(jnp.int32, (16, 1), 0)
    return jnp.where(row < 8, first.astype(f32), second.astype(f32))


def cells(block, frames):
    values = block.astype(f32)
    parts = []
    for frame in range(frames):
        for column in range(4):
            for wave in range(2):
                parts.append(values[wave, frame, :, column * C : (column + 1) * C])
    return jnp.concatenate(parts, axis=0)


def store_cells(ref, values):
    for frame in range(4):
        for wave in range(2):
            tiles = []
            for column in range(4):
                start = (frame * 4 + column) * 16 + wave * 8
                tiles.append(values[start : start + 8, :])
            ref[wave, frame] = jnp.concatenate(tiles, axis=1).astype(ref.dtype)


def times_rows(values, rows):
    n = values.shape[0] // 16
    return (values.reshape(n, 16, values.shape[1]) * rows[None]).reshape(values.shape)


def activate(values, gain):
    scale = lax.rsqrt(jnp.sum(values * values, axis=-1, keepdims=True) * (1.0 / C) + epsilon)
    normed = values * scale
    act = normed * gain
    sigma = 1.0 / (1.0 + jnp.exp(-act))
    return scale, normed, act, sigma


def store_shifted(padded, values):
    rows, width = values.shape
    frames = rows // 64
    at = lax.broadcasted_iota(jnp.int32, (rows, 1), 0) % 8
    zero = jnp.zeros((frames, 16, width), bf16)
    for shift in range(3):
        if shift == 0:
            moved = jnp.where(at == 0, 0.0, pltpu.roll(values, 1, axis=0))
        elif shift == 1:
            moved = values
        else:
            moved = jnp.where(at == 7, 0.0, pltpu.roll(values, rows - 1, axis=0))
        padded[shift, :, 0] = zero
        padded[shift, :, 5] = zero
        padded[shift, :, 1:5] = moved.astype(bf16).reshape(frames, 4, 16, width)


def fetch(pairs, semaphores):
    copies = [
        pltpu.make_async_copy(source, target, semaphores.at[i])
        for i, (source, target) in enumerate(pairs)
    ]
    for copy in copies:
        copy.start()
    for copy in copies:
        copy.wait()


def wave_before(block, lane):
    first, second = block[0].astype(f32), block[1].astype(f32)
    return jnp.stack([first, jnp.where(lane == 0, first, second)], axis=0)


def wave_after(block, lane):
    first, second = block[0].astype(f32), block[1].astype(f32)
    return jnp.stack([jnp.where(lane == LANES - 1, second, first), second], axis=0)


def hidden_frames(latent, before, gain, infos):
    own = cells(latent, 4)
    everything = jnp.concatenate([cells(before, 2), own], axis=0)
    scale, normed, act, sigma = activate(everything, gain)
    hidden = act * sigma
    same = per_row(infos[0][1], infos[1][1])
    return own, jnp.concatenate([times_rows(hidden[:128], same), hidden[128:]], axis=0)


def weight_kernel(
    numbers_ref, before_ref, latent_hbm, cotangent_hbm, gain_hbm,
    keep_ref, send_ref, latent_ref, cotangent_ref, gain_ref, semaphores, padded, grads,
):
    fetch(
        [(latent_hbm, latent_ref), (cotangent_hbm, cotangent_ref), (gain_hbm, gain_ref)], semaphores
    )
    lane, core, infos = scalars(numbers_ref)
    weight = 1.0 / per_row(infos[0][0], infos[1][0])
    before = wave_before(before_ref[...], lane)
    unused, hidden = hidden_frames(latent_ref[...], before, gain_ref[...], infos)
    store_shifted(padded, hidden)
    upstream = times_rows(cells(cotangent_ref[...], 4), weight)
    low = upstream[:, :128]
    high = jnp.concatenate([upstream[:, 128:], jnp.zeros((256, 64), f32)], axis=1)
    early = jnp.concatenate([low, high], axis=1).astype(bf16)
    late = jnp.concatenate([low, pltpu.roll(high, 64, axis=1)], axis=1).astype(bf16)
    for tap in range(27):
        t, i, j = tap // 9, (tap // 3) % 3, tap % 3
        patch = padded[i, t : t + 4, j : j + 4].reshape(256, C)
        part = lax.dot_general(
            patch, early if tap < 14 else late, (((0,), (0,)), ((), ())),
            preferred_element_type=f32,
        )
        grads[:, 24 * tap : 24 * tap + 24, :] = part.reshape(8, 24, 256)
    grads[:, 648:672, :] = jnp.zeros((8, 24, 256), f32)
    for y in range(NY):
        for ref, which in ((send_ref, 1 - core), (keep_ref, core)):
            d = 2 * y + which
            ref[0, y] = grads[d, 0:256, 0:128].astype(bf16)
            ref[1, y] = grads[d, 256:512, 0:128].astype(bf16)
            ref[2, y, 0:160] = grads[d, 512:672, 0:128].astype(bf16)
            ref[2, y, 160:256] = (grads[d, 0:96, 128:256] + grads[d, 336:432, 128:256]).astype(bf16)
            ref[3, y, 0:240] = (grads[d, 96:336, 128:256] + grads[d, 432:672, 128:256]).astype(bf16)
            ref[3, y, 240:256] = jnp.zeros((16, 128), bf16)


def share_kernel(share_ref, out_ref, flat):
    for tap in range(27):
        flat[12 * tap : 12 * tap + 12, :] = share_ref[tap].astype(f32)
    flat[324:336, :] = jnp.zeros((12, 2 * C), f32)
    block = flat[...].astype(bf16)
    for y in range(NY):
        out_ref[y] = block


def permutation(core):
    channel = lax.broadcasted_iota(jnp.int32, (C, 256), 0)
    place = lax.broadcasted_iota(jnp.int32, (C, 256), 1)
    h, e, r = place // 128, (place % 128) // 16, place % 16
    d = 2 * (e % 4) + jnp.where(e < 4, core, 1 - core)
    hit = jnp.logical_and(channel == 24 * d + 2 * r + h, r < 12)
    return jnp.where(hit, 1.0, 0.0).astype(bf16)


def unpack(own_ref, other_ref, rows_ref):
    for y in range(NY):
        rows_ref[y] = own_ref[y].astype(f32)
        rows_ref[NY + y] = other_ref[y].astype(f32)


def tap_matrix(rows_ref, tap):
    rows = jnp.concatenate([rows_ref[e, 12 * tap : 12 * tap + 16, :] for e in range(8)], axis=0)
    return jnp.concatenate([rows[:, :C], rows[:, C:]], axis=0).astype(bf16)


def adjoint_kernel(
    numbers_ref, after_ref, own_ref, other_ref, latent_hbm, cotangent_hbm, gain_hbm,
    latent_grad_ref, gain_part_ref, latent_ref, cotangent_ref, gain_ref, semaphores, wide, rows_ref,
):
    fetch(
        [(latent_hbm, latent_ref), (cotangent_hbm, cotangent_ref), (gain_hbm, gain_ref)], semaphores
    )
    lane, core, infos = scalars(numbers_ref)
    weight = 1.0 / per_row(infos[0][0], infos[1][0])
    following = per_row(infos[0][2], infos[1][2])
    unpack(own_ref, other_ref, rows_ref)
    upstream = times_rows(cells(cotangent_ref[...], 4), weight).astype(bf16).astype(f32)
    after = cells(wave_after(after_ref[...], lane), 2)
    later = times_rows(times_rows(after, weight), following)
    store_shifted(wide, jnp.concatenate([upstream, later], axis=0))
    hidden_grad = jnp.zeros((256, 256), f32)
    for tap in range(27):
        t, i, j = tap // 9, (tap // 3) % 3, tap % 3
        patch = wide[2 - i, 2 - t : 6 - t, 2 - j : 6 - j].reshape(256, C)
        hidden_grad = hidden_grad + lax.dot_general(
            patch, tap_matrix(rows_ref, tap), (((1,), (1,)), ((), ())), preferred_element_type=f32
        )
    order = permutation(core)
    coarse = hidden_grad.astype(bf16)
    fine = (hidden_grad - coarse.astype(f32)).astype(bf16)
    back = (((1,), (1,)), ((), ()))
    hidden_grad = lax.dot_general(
        coarse, order, back, preferred_element_type=f32
    ) + lax.dot_general(fine, order, back, preferred_element_type=f32)
    gain = gain_ref[...]
    scale, normed, act, sigma = activate(cells(latent_ref[...], 4), gain)
    act_grad = hidden_grad * sigma * (1.0 + act * (1.0 - sigma))
    gain_part = jnp.sum(act_grad * normed, axis=0, keepdims=True)
    inner = act_grad * gain
    mean = jnp.sum(inner * normed, axis=-1, keepdims=True) * (1.0 / C)
    store_cells(latent_grad_ref, upstream + scale * (inner - normed * mean))
    gain_part_ref[...] = jnp.zeros((8, 128), f32)
    gain_part_ref[0:1, :] = gain_part[:, :128]
    gain_part_ref[1:2, 0:64] = gain_part[:, 128:]


def forward_kernel(
    numbers_ref, before_ref, own_ref, other_ref, latent_hbm, gain_hbm,
    decoded_ref, latent_ref, gain_ref, semaphores, padded, rows_ref,
):
    fetch([(latent_hbm, latent_ref), (gain_hbm, gain_ref)], semaphores)
    lane, core, infos = scalars(numbers_ref)
    unpack(own_ref, other_ref, rows_ref)
    before = wave_before(before_ref[...], lane)
    latent, hidden = hidden_frames(latent_ref[...], before, gain_ref[...], infos)
    store_shifted(padded, jnp.dot(hidden.astype(bf16), permutation(core), preferred_element_type=f32))
    mixed = jnp.zeros((256, C), f32)
    for tap in range(27):
        t, i, j = tap // 9, (tap // 3) % 3, tap % 3
        patch = padded[i, t : t + 4, j : j + 4].reshape(256, 256)
        mixed = mixed + jnp.dot(patch, tap_matrix(rows_ref, tap), preferred_element_type=f32)
    store_cells(decoded_ref, latent + mixed)


def two_parts(gain):
    coarse = gain.astype(bf16).astype(f32)
    return jnp.concatenate([coarse, gain - coarse], axis=0)


def first_sum_kernel(pieces_ref, own_ref, other_ref, out_ref):
    gain = two_parts(own_ref[...] + other_ref[...]).astype(bf16)
    for y in range(NY):
        total = jnp.sum(pieces_ref[:, y].astype(f32), axis=0).astype(bf16)
        for part in range(NL):
            out_ref[NL * y + part, 0:64] = total[64 * part : 64 * part + 64]
            out_ref[NL * y + part, 64:80] = gain


def next_sum_kernel(pieces_ref, out_ref):
    total = jnp.sum(pieces_ref[...].astype(f32), axis=0)
    gain = two_parts(total[64:72] + total[72:80])
    block = jnp.concatenate([total[0:64], gain], axis=0).astype(bf16)
    for copy in range(out_ref.shape[0]):
        out_ref[copy] = block


def finish_kernel(parts_ref, out_ref, gain_ref, left, right):
    gain = jnp.zeros((8, 128), f32)
    for x in range(NX):
        both = parts_ref[NL * x, 64:80].astype(f32)
        gain = gain + both[0:8] + both[8:16]
    gain_ref[...] = jnp.concatenate([gain[0:1], gain[1:2, 0:64]], axis=1)
    rows = parts_ref[:, 0:64].astype(f32).reshape(1024, 128)
    low = rows[672:1008]
    left[...] = rows[0:672]
    right[0:336] = low
    right[336:672] = pltpu.roll(low, 64, axis=1)
    for tap in range(27):
        even, odd = pl.ds(24 * tap, 12, stride=2), pl.ds(24 * tap + 1, 12, stride=2)
        tiles = [left[even, :], right[even, :][:, :64], left[odd, :], right[odd, :][:, :64]]
        out_ref[tap] = jnp.concatenate(tiles, axis=1)


SPECS = {"s": pltpu.SMEM, "v": pltpu.VMEM, "h": pltpu.HBM}


def call(kernel, name, places, operands, out_shapes, scratch=()):
    return pl.pallas_call(
        kernel,
        name=name,
        out_shape=out_shapes,
        in_specs=[pl.BlockSpec(memory_space=SPECS[place]) for place in places],
        out_specs=jax.tree.map(lambda unused: pl.BlockSpec(memory_space=pltpu.VMEM), out_shapes),
        scratch_shapes=list(scratch),
        compiler_params=pltpu.CompilerParams(vmem_limit_bytes=VMEM_LIMIT),
    )(*operands)


def ring(by):
    return [(i, (i + by) % LANES) for i in range(LANES)]


def on_device(video_latents, cotangent, conv_weight, norm_gain, clip_lengths):
    shape = jax.ShapeDtypeStruct
    clip = ("x", "zh", "zl")
    latent = video_latents[0, :, 0]
    upstream_raw = cotangent[0, :, 0]
    gain = norm_gain.reshape(1, C)
    lane = (lax.axis_index("x") * NH + lax.axis_index("zh")) * NL + lax.axis_index("zl")
    place = jnp.stack([lane, lax.axis_index("core")]).astype(jnp.int32)
    numbers = jnp.concatenate([clip_lengths[0], place])

    share = call(
        share_kernel, "share", "v", (conv_weight.reshape(27, 12, 2 * C),),
        shape((NY, 336, 2 * C), bf16), [pltpu.VMEM((336, 2 * C), f32)],
    )
    last, share = lax.optimization_barrier((latent[:, 2:], share))
    own = lax.all_to_all(share, "y", 0, 0, tiled=True)
    before = lax.ppermute(last, clip, ring(1))
    after = lax.ppermute(upstream_raw[:, :2], clip, ring(-1))

    inputs = [
        pltpu.VMEM(latent.shape, bf16), pltpu.VMEM(latent.shape, bf16), pltpu.VMEM((1, C), f32),
        pltpu.SemaphoreType.DMA((3,)),
    ]
    piece = shape((NX, NY, 256, 128), bf16)
    keep, send = call(
        weight_kernel, "weight_grad", "svhhh", (numbers, before, latent, upstream_raw, gain),
        (piece, piece),
        inputs + [pltpu.VMEM((3, 6, 6, 16, C), bf16), pltpu.VMEM((8, 672, 256), f32)],
    )
    swap = [(0, 1), (1, 0)]
    send, own = lax.optimization_barrier((send, own))
    received = lax.ppermute(send, "core", swap)
    pair = (keep.astype(f32) + received.astype(f32)).astype(bf16)
    other = lax.ppermute(own, "core", swap)
    pieces = lax.all_to_all(pair, "x", 0, 0, tiled=True)

    latent_grad, gain_part = call(
        adjoint_kernel, "adjoint", "svvvhhh",
        (numbers, after, own, other, latent, upstream_raw, gain),
        (shape(latent.shape, bf16), shape((8, 128), f32)),
        inputs + [pltpu.VMEM((3, 6, 6, 16, C), bf16), pltpu.VMEM((8, 336, 2 * C), f32)],
    )
    gain_other = lax.ppermute(gain_part, "core", swap)
    blocks = call(
        first_sum_kernel, "first_sum", "vvv", (pieces, gain_part, gain_other),
        shape((NY * NL, 80, 128), bf16),
    )
    blocks, other = lax.optimization_barrier((blocks, other))
    decoded = call(
        forward_kernel, "forward", "svvvhh", (numbers, before, own, other, latent, gain),
        shape(latent.shape, bf16),
        [
            pltpu.VMEM(latent.shape, bf16), pltpu.VMEM((1, C), f32), pltpu.SemaphoreType.DMA((2,)),
            pltpu.VMEM((3, 6, 6, 16, 256), bf16), pltpu.VMEM((8, 336, 2 * C), f32),
        ],
    )

    blocks = lax.all_to_all(blocks, ("y", "zl"), 0, 0, tiled=True)
    blocks = call(next_sum_kernel, "second_sum", "v", (blocks,), shape((NH, 80, 128), bf16))
    blocks = lax.all_to_all(blocks, "zh", 0, 0, tiled=True)
    blocks = call(next_sum_kernel, "third_sum", "v", (blocks,), shape((NX * NL, 80, 128), bf16))
    blocks = lax.all_to_all(blocks, ("x", "zl"), 0, 0, tiled=True)
    weight_grad, gain_grad = call(
        finish_kernel, "finish", "v", (blocks,),
        (shape((27, 12, 2 * C), f32), shape((1, C), f32)), [pltpu.VMEM((672, 128), f32)] * 2,
    )
    return (
        decoded[None, :, None],
        latent_grad[None, :, None],
        weight_grad.reshape(3, 3, 3, 12, 2 * C),
        gain_grad.reshape(C),
    )


def solution(mesh):
    axes = Mesh(mesh.devices.reshape(NX, NH, NL, NY, NCORE), ("x", "zh", "zl", "y", "core"))
    dp, clip = ("y", "core"), ("x", "zh", "zl")
    data = P(dp, None, clip, None, None, None)
    kernel = P(None, None, None, dp, None)
    return jax.shard_map(
        on_device,
        mesh=axes,
        in_specs=(data, data, kernel, P(), P(dp, None)),
        out_specs=(data, data, kernel, P()),
        check_vma=False,
    )
```

```python
import jax
import jax.numpy as jnp
from jax import lax
from jax.experimental import pallas as pl
from jax.experimental.pallas import tpu as pltpu
from jax.sharding import Mesh, PartitionSpec as P

epsilon = 1e-06
bf16 = jnp.bfloat16
f32 = jnp.float32
C = 192
NX, NH, NL, NY, NCORE = 4, 4, 4, 4, 2
LANES = NX * NH * NL
VMEM_LIMIT = 24 * 1024 * 1024


def scalars(numbers_ref):
    count = numbers_ref.shape[0] - 2
    lane = numbers_ref[count]
    infos = []
    for wave in range(2):
        q = wave * LANES + lane
        begin = jnp.int32(0)
        length = jnp.int32(0)
        starts = jnp.int32(0)
        next_starts = jnp.int32(0)
        for k in range(count):
            own = numbers_ref[k]
            end = begin + own
            inside = jnp.logical_and(q >= begin, q < end)
            length = length + jnp.where(inside, own, 0)
            starts = starts + jnp.where(q == begin, 1, 0)
            next_starts = next_starts + jnp.where(q + 1 == begin, 1, 0)
            begin = end
        same = jnp.where(starts == 0, 1, 0)
        following = jnp.where(
            jnp.logical_and(next_starts == 0, q + 1 < 2 * LANES), 1, 0
        )
        infos.append((length, same, following))
    return lane, numbers_ref[count + 1], infos


def per_row(first, second):
    row = lax.broadcasted_iota(jnp.int32, (16, 1), 0)
    return jnp.where(row < 8, first.astype(f32), second.astype(f32))


def cells(block, frames):
    values = block.astype(f32)
    parts = []
    for frame in range(frames):
        for column in range(4):
            for wave in range(2):
                parts.append(values[wave, frame, :, column * C : (column + 1) * C])
    return jnp.concatenate(parts, axis=0)


def store_cells(ref, values):
    for frame in range(4):
        for wave in range(2):
            tiles = []
            for column in range(4):
                start = (frame * 4 + column) * 16 + wave * 8
                tiles.append(values[start : start + 8, :])
            ref[wave, frame] = jnp.concatenate(tiles, axis=1).astype(ref.dtype)


def times_rows(values, rows):
    n = values.shape[0] // 16
    return (values.reshape(n, 16, values.shape[1]) * rows[None]).reshape(values.shape)


def activate(values, gain):
    scale = lax.rsqrt(jnp.sum(values * values, axis=-1, keepdims=True) * (1.0 / C) + epsilon)
    normed = values * scale
    act = normed * gain
    sigma = 1.0 / (1.0 + jnp.exp(-act))
    return scale, normed, act, sigma


def store_shifted(padded, values):
    rows, width = values.shape
    frames = rows // 64
    at = lax.broadcasted_iota(jnp.int32, (rows, 1), 0) % 8
    zero = jnp.zeros((frames, 16, width), bf16)
    for shift in range(3):
        if shift == 0:
            moved = jnp.where(at == 0, 0.0, pltpu.roll(values, 1, axis=0))
        elif shift == 1:
            moved = values
        else:
            moved = jnp.where(at == 7, 0.0, pltpu.roll(values, rows - 1, axis=0))
        padded[shift, :, 0] = zero
        padded[shift, :, 5] = zero
        padded[shift, :, 1:5] = moved.astype(bf16).reshape(frames, 4, 16, width)


def fetch(pairs, semaphores):
    copies = [
        pltpu.make_async_copy(source, target, semaphores.at[i])
        for i, (source, target) in enumerate(pairs)
    ]
    for copy in copies:
        copy.start()
    for copy in copies:
        copy.wait()


def wave_before(block, lane):
    first, second = block[0].astype(f32), block[1].astype(f32)
    return jnp.stack([first, jnp.where(lane == 0, first, second)], axis=0)


def wave_after(block, lane):
    first, second = block[0].astype(f32), block[1].astype(f32)
    return jnp.stack([jnp.where(lane == LANES - 1, second, first), second], axis=0)


def hidden_frames(latent, before, gain, infos):
    own = cells(latent, 4)
    everything = jnp.concatenate([cells(before, 2), own], axis=0)
    scale, normed, act, sigma = activate(everything, gain)
    hidden = act * sigma
    same = per_row(infos[0][1], infos[1][1])
    return own, jnp.concatenate([times_rows(hidden[:128], same), hidden[128:]], axis=0)


def weight_kernel(
    numbers_ref, before_ref, latent_hbm, cotangent_hbm, gain_hbm,
    keep_ref, send_ref, latent_ref, cotangent_ref, gain_ref, semaphores, padded, grads,
):
    fetch(
        [(latent_hbm, latent_ref), (cotangent_hbm, cotangent_ref), (gain_hbm, gain_ref)], semaphores
    )
    lane, core, infos = scalars(numbers_ref)
    weight = 1.0 / per_row(infos[0][0], infos[1][0])
    before = wave_before(before_ref[...], lane)
    unused, hidden = hidden_frames(latent_ref[...], before, gain_ref[...], infos)
    store_shifted(padded, hidden)
    upstream = times_rows(cells(cotangent_ref[...], 4), weight)
    low = upstream[:, :128]
    high = jnp.concatenate([upstream[:, 128:], jnp.zeros((256, 64), f32)], axis=1)
    early = jnp.concatenate([low, high], axis=1).astype(bf16)
    late = jnp.concatenate([low, pltpu.roll(high, 64, axis=1)], axis=1).astype(bf16)
    for tap in range(27):
        t, i, j = tap // 9, (tap // 3) % 3, tap % 3
        patch = padded[i, t : t + 4, j : j + 4].reshape(256, C)
        part = lax.dot_general(
            patch, early if tap < 14 else late, (((0,), (0,)), ((), ())),
            preferred_element_type=f32,
        )
        grads[:, 24 * tap : 24 * tap + 24, :] = part.reshape(8, 24, 256)
    grads[:, 648:672, :] = jnp.zeros((8, 24, 256), f32)
    for y in range(NY):
        for ref, which in ((send_ref, 1 - core), (keep_ref, core)):
            d = 2 * y + which
            at = (y % 2, y // 2)
            mixed = grads[d, 0:336, 128:256] + grads[d, 336:672, 128:256]
            ref[(0, *at)] = grads[d, 0:256, 0:128].astype(bf16)
            ref[(1, *at)] = grads[d, 256:512, 0:128].astype(bf16)
            ref[(2, *at, slice(0, 160))] = grads[d, 512:672, 0:128].astype(bf16)
            ref[(2, *at, slice(160, 256))] = mixed[0:96].astype(bf16)
            ref[(3, *at, slice(0, 240))] = mixed[96:336].astype(bf16)
            ref[(3, *at, slice(240, 256))] = jnp.zeros((16, 128), bf16)


def pair_kernel(keep_ref, received_ref, out_ref):
    out_ref[...] = (keep_ref[...].astype(f32) + received_ref[...].astype(f32)).astype(bf16)


def share_kernel(share_ref, out_ref, flat):
    for tap in range(27):
        flat[12 * tap : 12 * tap + 12, :] = share_ref[tap].astype(f32)
    flat[324:336, :] = jnp.zeros((12, 2 * C), f32)
    block = flat[...].astype(bf16)
    for y in range(NY):
        out_ref[y] = block


def permutation(core):
    channel = lax.broadcasted_iota(jnp.int32, (C, 256), 0)
    place = lax.broadcasted_iota(jnp.int32, (C, 256), 1)
    h, e, r = place // 128, (place % 128) // 16, place % 16
    d = 2 * (e % 4) + jnp.where(e < 4, core, 1 - core)
    hit = jnp.logical_and(channel == 24 * d + 2 * r + h, r < 12)
    return jnp.where(hit, 1.0, 0.0).astype(bf16)


def unpack(own_ref, other_ref, rows_ref):
    for y in range(NY):
        rows_ref[y] = own_ref[y].astype(f32)
        rows_ref[NY + y] = other_ref[y].astype(f32)


def tap_matrix(rows_ref, tap):
    parts = [rows_ref[e, 12 * tap : 12 * tap + 16, :].astype(bf16) for e in range(8)]
    rows = jnp.concatenate(parts, axis=0)
    return jnp.concatenate([rows[:, :C], rows[:, C:]], axis=0)


def adjoint_kernel(
    numbers_ref, after_ref, own_ref, other_ref, latent_hbm, cotangent_hbm, gain_hbm,
    latent_grad_ref, gain_part_ref, latent_ref, cotangent_ref, gain_ref, semaphores, wide, rows_ref,
):
    fetch(
        [(latent_hbm, latent_ref), (cotangent_hbm, cotangent_ref), (gain_hbm, gain_ref)], semaphores
    )
    lane, core, infos = scalars(numbers_ref)
    weight = 1.0 / per_row(infos[0][0], infos[1][0])
    following = per_row(infos[0][2], infos[1][2])
    unpack(own_ref, other_ref, rows_ref)
    upstream = times_rows(cells(cotangent_ref[...], 4), weight).astype(bf16).astype(f32)
    after = cells(wave_after(after_ref[...], lane), 2)
    later = times_rows(times_rows(after, weight), following)
    store_shifted(wide, jnp.concatenate([upstream, later], axis=0))
    hidden_grad = jnp.zeros((256, 256), f32)
    for tap in range(27):
        t, i, j = tap // 9, (tap // 3) % 3, tap % 3
        patch = wide[2 - i, 2 - t : 6 - t, 2 - j : 6 - j].reshape(256, C)
        hidden_grad = hidden_grad + lax.dot_general(
            patch, tap_matrix(rows_ref, tap), (((1,), (1,)), ((), ())), preferred_element_type=f32
        )
    order = permutation(core)
    coarse = hidden_grad.astype(bf16)
    fine = (hidden_grad - coarse.astype(f32)).astype(bf16)
    back = (((1,), (1,)), ((), ()))
    hidden_grad = lax.dot_general(
        coarse, order, back, preferred_element_type=f32
    ) + lax.dot_general(fine, order, back, preferred_element_type=f32)
    gain = gain_ref[...]
    scale, normed, act, sigma = activate(cells(latent_ref[...], 4), gain)
    act_grad = hidden_grad * sigma * (1.0 + act * (1.0 - sigma))
    gain_part = jnp.sum(act_grad * normed, axis=0, keepdims=True)
    inner = act_grad * gain
    mean = jnp.sum(inner * normed, axis=-1, keepdims=True) * (1.0 / C)
    store_cells(latent_grad_ref, upstream + scale * (inner - normed * mean))
    gain_part_ref[...] = jnp.zeros((8, 128), f32)
    gain_part_ref[0:1, :] = gain_part[:, :128]
    gain_part_ref[1:2, 0:64] = gain_part[:, 128:]


def forward_kernel(
    numbers_ref, before_ref, own_ref, other_ref, latent_hbm, gain_hbm,
    decoded_ref, latent_ref, gain_ref, semaphores, padded, rows_ref,
):
    fetch([(latent_hbm, latent_ref), (gain_hbm, gain_ref)], semaphores)
    lane, core, infos = scalars(numbers_ref)
    unpack(own_ref, other_ref, rows_ref)
    before = wave_before(before_ref[...], lane)
    latent, hidden = hidden_frames(latent_ref[...], before, gain_ref[...], infos)
    store_shifted(padded, jnp.dot(hidden.astype(bf16), permutation(core), preferred_element_type=f32))
    mixed = jnp.zeros((256, C), f32)
    for tap in range(27):
        t, i, j = tap // 9, (tap // 3) % 3, tap % 3
        patch = padded[i, t : t + 4, j : j + 4].reshape(256, 256)
        mixed = mixed + jnp.dot(patch, tap_matrix(rows_ref, tap), preferred_element_type=f32)
    store_cells(decoded_ref, latent + mixed)


def two_parts(gain):
    coarse = gain.astype(bf16).astype(f32)
    return jnp.concatenate([coarse, gain - coarse], axis=0)


def add_kernel(own_ref, other_ref, out_ref):
    out_ref[...] = own_ref[...] + other_ref[...]


def first_sum_kernel(pieces_ref, own_ref, other_ref, out_ref):
    gain = two_parts(own_ref[...] + other_ref[...]).astype(bf16)
    total = jnp.sum(pieces_ref[...].astype(f32), axis=0).astype(bf16)
    for part in range(2 * NL):
        out_ref[part, 0:64] = total[64 * part : 64 * part + 64]
        out_ref[part, 64:80] = gain


def next_sum_kernel(pieces_ref, out_ref):
    total = jnp.sum(pieces_ref[...].astype(f32), axis=0)
    gain = two_parts(total[64:72] + total[72:80])
    block = jnp.concatenate([total[0:64], gain], axis=0).astype(bf16)
    for copy in range(out_ref.shape[0]):
        out_ref[copy] = block


def finish_kernel(parts_ref, out_ref, gain_ref, left, right):
    gain = jnp.zeros((8, 128), f32)
    for x in range(NX):
        both = parts_ref[NL * x, 64:80].astype(f32)
        gain = gain + both[0:8] + both[8:16]
    gain_ref[...] = jnp.concatenate([gain[0:1], gain[1:2, 0:64]], axis=1)
    rows = parts_ref[:, 0:64].astype(f32).reshape(1024, 128)
    low = rows[672:1008]
    left[...] = rows[0:672]
    right[0:336] = low
    right[336:672] = pltpu.roll(low, 64, axis=1)
    for tap in range(27):
        even, odd = pl.ds(24 * tap, 12, stride=2), pl.ds(24 * tap + 1, 12, stride=2)
        tiles = [left[even, :], right[even, :][:, :64], left[odd, :], right[odd, :][:, :64]]
        out_ref[tap] = jnp.concatenate(tiles, axis=1)


SPECS = {"s": pltpu.SMEM, "v": pltpu.VMEM, "h": pltpu.HBM}


def call(kernel, name, places, operands, out_shapes, scratch=()):
    return pl.pallas_call(
        kernel,
        name=name,
        out_shape=out_shapes,
        in_specs=[pl.BlockSpec(memory_space=SPECS[place]) for place in places],
        out_specs=jax.tree.map(lambda unused: pl.BlockSpec(memory_space=pltpu.VMEM), out_shapes),
        scratch_shapes=list(scratch),
        compiler_params=pltpu.CompilerParams(vmem_limit_bytes=VMEM_LIMIT),
    )(*operands)


def ring(by):
    return [(i, (i + by) % LANES) for i in range(LANES)]


def on_device(video_latents, cotangent, conv_weight, norm_gain, clip_lengths):
    shape = jax.ShapeDtypeStruct
    clip = ("x", "zh", "zl")
    latent = video_latents[0, :, 0]
    upstream_raw = cotangent[0, :, 0]
    gain = norm_gain.reshape(1, C)
    lane = (lax.axis_index("x") * NH + lax.axis_index("zh")) * NL + lax.axis_index("zl")
    place = jnp.stack([lane, lax.axis_index("core")]).astype(jnp.int32)
    numbers = jnp.concatenate([clip_lengths[0], place])

    share = call(
        share_kernel, "share", "v", (conv_weight.reshape(27, 12, 2 * C),),
        shape((NY, 336, 2 * C), bf16), [pltpu.VMEM((336, 2 * C), f32)],
    )
    latest, share = lax.optimization_barrier((latent, share))
    own = lax.all_to_all(share, ("yh", "yl"), 0, 0, tiled=True)
    before = lax.ppermute(latest[:, 2:], clip, ring(1))
    after = lax.ppermute(upstream_raw[:, :2], clip, ring(-1))

    inputs = [
        pltpu.VMEM(latent.shape, bf16), pltpu.VMEM(latent.shape, bf16), pltpu.VMEM((1, C), f32),
        pltpu.SemaphoreType.DMA((3,)),
    ]
    piece = shape((NX, 2, 2, 256, 128), bf16)
    keep, send = call(
        weight_kernel, "weight_grad", "svhhh", (numbers, before, latent, upstream_raw, gain),
        (piece, piece),
        inputs + [pltpu.VMEM((3, 6, 6, 16, C), bf16), pltpu.VMEM((8, 672, 256), f32)],
    )
    swap = [(0, 1), (1, 0)]
    send, own, after = lax.optimization_barrier((send, own, after))
    received = lax.ppermute(send, "core", swap)
    other = lax.ppermute(own, "core", swap)
    pair = call(pair_kernel, "pair", "vv", (keep, received), piece)
    pieces = lax.all_to_all(pair.reshape(NX * 2, 512, 128), ("x", "yl"), 0, 0, tiled=True)

    latent_grad, gain_part = call(
        adjoint_kernel, "adjoint", "svvvhhh",
        (numbers, after, own, other, latent, upstream_raw, gain),
        (shape(latent.shape, bf16), shape((8, 128), f32)),
        inputs + [pltpu.VMEM((3, 6, 6, 16, C), bf16), pltpu.VMEM((8, 336, 2 * C), f32)],
    )
    gain_other = lax.ppermute(gain_part, "core", swap)
    both = call(add_kernel, "gain_pair", "vv", (gain_part, gain_other), shape((8, 128), f32))
    near = lax.ppermute(both, "yl", swap)
    blocks = call(
        first_sum_kernel, "first_sum", "vvv", (pieces, both, near),
        shape((2 * NL, 80, 128), bf16),
    )
    blocks = lax.all_to_all(blocks, ("yh", "zl"), 0, 0, tiled=True)
    blocks = call(next_sum_kernel, "second_sum", "v", (blocks,), shape((NH, 80, 128), bf16))
    blocks, other = lax.optimization_barrier((blocks, other))
    blocks = lax.all_to_all(blocks, "zh", 0, 0, tiled=True)
    decoded = call(
        forward_kernel, "forward", "svvvhh", (numbers, before, own, other, latent, gain),
        shape(latent.shape, bf16),
        [
            pltpu.VMEM(latent.shape, bf16), pltpu.VMEM((1, C), f32), pltpu.SemaphoreType.DMA((2,)),
            pltpu.VMEM((3, 6, 6, 16, 256), bf16), pltpu.VMEM((8, 336, 2 * C), f32),
        ],
    )

    blocks = call(next_sum_kernel, "third_sum", "v", (blocks,), shape((NX * NL, 80, 128), bf16))
    blocks = lax.all_to_all(blocks, ("x", "zl"), 0, 0, tiled=True)
    weight_grad, gain_grad = call(
        finish_kernel, "finish", "v", (blocks,),
        (shape((27, 12, 2 * C), f32), shape((1, C), f32)), [pltpu.VMEM((672, 128), f32)] * 2,
    )
    return (
        decoded[None, :, None],
        latent_grad[None, :, None],
        weight_grad.reshape(3, 3, 3, 12, 2 * C),
        gain_grad.reshape(C),
    )


def solution(mesh):
    names = ("x", "zh", "zl", "yh", "yl", "core")
    axes = Mesh(mesh.devices.reshape(NX, NH, NL, 2, 2, NCORE), names)
    dp, clip = ("yh", "yl", "core"), ("x", "zh", "zl")
    data = P(dp, None, clip, None, None, None)
    kernel = P(None, None, None, dp, None)
    return jax.shard_map(
        on_device,
        mesh=axes,
        in_specs=(data, data, kernel, P(), P(dp, None)),
        out_specs=(data, data, kernel, P()),
        check_vma=False,
    )
```

```python
import jax
import jax.numpy as jnp
from jax import lax
from jax.experimental import pallas as pl
from jax.experimental.pallas import tpu as pltpu
from jax.sharding import Mesh, PartitionSpec as P

epsilon = 1e-06
bf16 = jnp.bfloat16
f32 = jnp.float32
C = 192
NX, NH, NL, NY, NCORE = 4, 4, 4, 4, 2
LANES = NX * NH * NL
VMEM_LIMIT = 24 * 1024 * 1024


def scalars(numbers_ref):
    count = numbers_ref.shape[0] - 2
    lane = numbers_ref[count]
    infos = []
    for wave in range(2):
        q = wave * LANES + lane
        begin = jnp.int32(0)
        length = jnp.int32(0)
        starts = jnp.int32(0)
        next_starts = jnp.int32(0)
        for k in range(count):
            own = numbers_ref[k]
            end = begin + own
            inside = jnp.logical_and(q >= begin, q < end)
            length = length + jnp.where(inside, own, 0)
            starts = starts + jnp.where(q == begin, 1, 0)
            next_starts = next_starts + jnp.where(q + 1 == begin, 1, 0)
            begin = end
        same = jnp.where(starts == 0, 1, 0)
        following = jnp.where(
            jnp.logical_and(next_starts == 0, q + 1 < 2 * LANES), 1, 0
        )
        infos.append((length, same, following))
    return lane, numbers_ref[count + 1], infos


def per_row(first, second):
    row = lax.broadcasted_iota(jnp.int32, (16, 1), 0)
    return jnp.where(row < 8, first.astype(f32), second.astype(f32))


def cells(block, frames):
    values = block.astype(f32)
    parts = []
    for frame in range(frames):
        for column in range(4):
            for wave in range(2):
                parts.append(values[wave, frame, :, column * C : (column + 1) * C])
    return jnp.concatenate(parts, axis=0)


def store_cells(ref, values):
    for frame in range(4):
        for wave in range(2):
            tiles = []
            for column in range(4):
                start = (frame * 4 + column) * 16 + wave * 8
                tiles.append(values[start : start + 8, :])
            ref[wave, frame] = jnp.concatenate(tiles, axis=1).astype(ref.dtype)


def times_rows(values, rows):
    n = values.shape[0] // 16
    return (values.reshape(n, 16, values.shape[1]) * rows[None]).reshape(values.shape)


def activate(values, gain):
    scale = lax.rsqrt(jnp.sum(values * values, axis=-1, keepdims=True) * (1.0 / C) + epsilon)
    normed = values * scale
    act = normed * gain
    sigma = 1.0 / (1.0 + jnp.exp(-act))
    return scale, normed, act, sigma


def store_shifted(padded, values):
    rows, width = values.shape
    frames = rows // 64
    at = lax.broadcasted_iota(jnp.int32, (rows, 1), 0) % 8
    zero = jnp.zeros((frames, 16, width), bf16)
    for shift in range(3):
        if shift == 0:
            moved = jnp.where(at == 0, 0.0, pltpu.roll(values, 1, axis=0))
        elif shift == 1:
            moved = values
        else:
            moved = jnp.where(at == 7, 0.0, pltpu.roll(values, rows - 1, axis=0))
        padded[shift, :, 0] = zero
        padded[shift, :, 5] = zero
        padded[shift, :, 1:5] = moved.astype(bf16).reshape(frames, 4, 16, width)


def wave_before(block, lane):
    first, second = block[0].astype(f32), block[1].astype(f32)
    return jnp.stack([first, jnp.where(lane == 0, first, second)], axis=0)


def wave_after(block, lane):
    first, second = block[0].astype(f32), block[1].astype(f32)
    return jnp.stack([jnp.where(lane == LANES - 1, second, first), second], axis=0)


def prepare_kernel(numbers_ref, latent_ref, cotangent_ref, gain_ref, both_ref):
    lane, core, infos = scalars(numbers_ref)
    weight = 1.0 / per_row(infos[0][0], infos[1][0])
    latent = cells(latent_ref[...], 4)
    unused, unused, act, sigma = activate(latent, gain_ref[...])
    both_ref[0:256] = (act * sigma).astype(bf16)
    both_ref[256:512] = times_rows(cells(cotangent_ref[...], 4), weight).astype(bf16)
    both_ref[512:768] = latent.astype(bf16)


def pack_kernel(numbers_ref, both_ref, before_ref, after_ref, gain_ref, out_ref):
    lane, core, infos = scalars(numbers_ref)
    weight = 1.0 / per_row(infos[0][0], infos[1][0])
    same = per_row(infos[0][1], infos[1][1])
    following = per_row(infos[0][2], infos[1][2])
    out_ref[0:768] = both_ref[...]
    unused, unused, act, sigma = activate(cells(wave_before(before_ref, lane), 2), gain_ref[...])
    out_ref[768:896] = times_rows(act * sigma, same).astype(bf16)
    after = times_rows(cells(wave_after(after_ref, lane), 2), weight)
    out_ref[896:1024] = times_rows(after, following).astype(bf16)


def selection(core):
    channel = lax.broadcasted_iota(jnp.int32, (C, 128), 0)
    place = lax.broadcasted_iota(jnp.int32, (C, 128), 1)
    hit = jnp.logical_and(channel == 24 * (2 * (place // 24) + core) + place % 24, place < 96)
    return jnp.where(hit, 1.0, 0.0).astype(bf16)


def weight_kernel(place_ref, own_ref, other_ref, out_hbm, wide, grads, out_ref, semaphores):
    core = place_ref[1]
    select = selection(core)
    hidden = []
    for r, block in enumerate((own_ref, other_ref)):
        hidden.append(jnp.dot(block[0:256], select, preferred_element_type=f32))
        upstream = jnp.concatenate([block[256:512], block[896:1024]], axis=0).astype(f32)
        blank = jnp.zeros((384, 64), f32)
        store_shifted(wide.at[r], jnp.concatenate([upstream, blank], axis=1))
    hidden = jnp.transpose(jnp.concatenate(hidden, axis=0)).astype(bf16)
    copies = []

    def send(x):
        for y in range(NY):
            target = out_hbm.at[x, y % 2, y // 2]
            copy = pltpu.make_async_copy(out_ref.at[x, y], target, semaphores.at[NY * x + y])
            copy.start()
            copies.append(copy)

    def high_half(y, start, stop):
        early = grads[y, start:stop, 128:256]
        return (early + grads[y, 336 + start : 336 + stop, 128:256]).astype(bf16)

    for tap in range(27):
        t, i, j = tap // 9, (tap // 3) % 3, tap % 3
        patch = [
            wide[r, 2 - i, 2 - t : 6 - t, 2 - j : 6 - j].reshape(256, 256) for r in range(2)
        ]
        part = jnp.dot(hidden, jnp.concatenate(patch, axis=0), preferred_element_type=f32)[:96]
        rows = slice(24 * tap, 24 * tap + 24)
        grads[:, rows, 0:128] = part[:, :128].reshape(NY, 24, 128)
        high = part[:, 128:] if tap < 14 else pltpu.roll(part[:, 128:], 64, axis=1)
        grads[:, rows, 128:256] = high.reshape(NY, 24, 128)
        if tap == 10 or tap == 21:
            x = tap // 20
            for y in range(NY):
                out_ref[x, y] = grads[y, 256 * x : 256 * x + 256, 0:128].astype(bf16)
            send(x)
        if tap == 24:
            for y in range(NY):
                out_ref[2, y] = high_half(y, 0, 256)
            send(2)
    grads[:, 648:672, :] = jnp.zeros((NY, 24, 256), f32)
    for y in range(NY):
        out_ref[3, y, 0:160] = grads[y, 512:672, 0:128].astype(bf16)
        out_ref[3, y, 160:240] = high_half(y, 256, 336)
        out_ref[3, y, 240:256] = jnp.zeros((16, 128), bf16)
    send(3)
    for copy in copies:
        copy.wait()


def share_kernel(share_ref, out_ref, flat):
    for tap in range(27):
        flat[12 * tap : 12 * tap + 12, :] = share_ref[tap].astype(f32)
    flat[324:336, :] = jnp.zeros((12, 2 * C), f32)
    block = flat[...].astype(bf16)
    for y in range(NY):
        out_ref[y] = block


def permutation(core):
    channel = lax.broadcasted_iota(jnp.int32, (C, 128), 0)
    place = lax.broadcasted_iota(jnp.int32, (C, 128), 1)
    h, y, r = place // 64, (place % 64) // 16, place % 16
    hit = jnp.logical_and(channel == 24 * (2 * y + core) + 2 * r + h, r < 12)
    return jnp.where(hit, 1.0, 0.0).astype(bf16)


def split_dot(values, matrix, dimensions):
    total = 0.0
    for unused in range(3):
        part = values.astype(bf16)
        values = values - part.astype(f32)
        total = total + lax.dot_general(part, matrix, dimensions, preferred_element_type=f32)
    return total


FORTH = (((1,), (0,)), ((), ()))
BACK = (((1,), (1,)), ((), ()))


def unpack(shares_ref, rows_ref):
    for y in range(NY):
        rows_ref[y] = shares_ref[y].astype(f32)


def tap_matrix(rows_ref, tap):
    parts = [rows_ref[y, 12 * tap : 12 * tap + 16, :].astype(bf16) for y in range(NY)]
    rows = jnp.concatenate(parts, axis=0)
    return jnp.concatenate([rows[:, :C], rows[:, C:]], axis=0)


def adjoint_kernel(
    place_ref, own_ref, other_ref, shares_ref, gain_ref,
    own_grad_ref, other_grad_ref, gain_part_ref, wide, rows_ref,
):
    core = place_ref[1]
    unpack(shares_ref, rows_ref)
    order = permutation(core)
    factors = []
    for r, block in enumerate((own_ref, other_ref)):
        upstream = jnp.concatenate([block[256:512], block[896:1024]], axis=0).astype(f32)
        store_shifted(wide.at[r], upstream)
        unused, normed, act, sigma = activate(block[512:768].astype(f32), gain_ref[...])
        factors.append(sigma * (1.0 + act * (1.0 - sigma)) * normed)
    factors = split_dot(jnp.concatenate(factors, axis=0), order, FORTH)
    hidden_grad = jnp.zeros((512, 128), f32)
    for tap in range(27):
        t, i, j = tap // 9, (tap // 3) % 3, tap % 3
        patch = [
            wide[r, 2 - i, 2 - t : 6 - t, 2 - j : 6 - j].reshape(256, C) for r in range(2)
        ]
        hidden_grad = hidden_grad + lax.dot_general(
            jnp.concatenate(patch, axis=0), tap_matrix(rows_ref, tap), BACK,
            preferred_element_type=f32,
        )
    own_grad_ref[...] = hidden_grad[:256]
    other_grad_ref[...] = hidden_grad[256:]
    gain_part = jnp.sum(hidden_grad * factors, axis=0, keepdims=True)
    gain_part = split_dot(gain_part, order, BACK)
    gain_part_ref[...] = jnp.zeros((8, 128), f32)
    gain_part_ref[0:1, :] = gain_part[:, :128]
    gain_part_ref[1:2, 0:64] = gain_part[:, 128:]


def forward_kernel(
    place_ref, own_ref, other_ref, shares_ref, other_grad_ref, mixed_ref, back_ref, padded, rows_ref
):
    core = place_ref[1]
    unpack(shares_ref, rows_ref)
    order = permutation(core)
    for r, block in enumerate((own_ref, other_ref)):
        hidden = jnp.concatenate([block[768:896], block[0:256]], axis=0)
        store_shifted(padded.at[r], jnp.dot(hidden, order, preferred_element_type=f32))
    mixed = jnp.zeros((512, C), f32)
    for tap in range(27):
        t, i, j = tap // 9, (tap // 3) % 3, tap % 3
        patch = [padded[r, i, t : t + 4, j : j + 4].reshape(256, 128) for r in range(2)]
        mixed = mixed + jnp.dot(
            jnp.concatenate(patch, axis=0), tap_matrix(rows_ref, tap), preferred_element_type=f32
        )
    mixed_ref[...] = mixed[:256]
    back_ref[:, 0:128] = other_grad_ref[...]
    back_ref[:, 128:320] = mixed[256:]
    back_ref[:, 320:384] = jnp.zeros((256, 64), f32)


def output_kernel(
    place_ref, both_ref, own_grad_ref, mixed_ref, back_ref, gain_ref, decoded_ref, latent_grad_ref
):
    core = place_ref[1]
    latent = both_ref[512:768].astype(f32)
    store_cells(decoded_ref, latent + (mixed_ref[...] + back_ref[:, 128:320]))
    hidden_grad = split_dot(own_grad_ref[...], permutation(core), BACK) + split_dot(
        back_ref[:, 0:128], permutation(1 - core), BACK
    )
    gain = gain_ref[...]
    scale, normed, act, sigma = activate(latent, gain)
    inner = hidden_grad * sigma * (1.0 + act * (1.0 - sigma)) * gain
    mean = jnp.sum(inner * normed, axis=-1, keepdims=True) * (1.0 / C)
    upstream = both_ref[256:512].astype(f32)
    store_cells(latent_grad_ref, upstream + scale * (inner - normed * mean))


def two_parts(gain):
    coarse = gain.astype(bf16).astype(f32)
    return jnp.concatenate([coarse, gain - coarse], axis=0)


def add_kernel(own_ref, other_ref, out_ref):
    out_ref[...] = own_ref[...] + other_ref[...]


def first_sum_kernel(pieces_ref, own_ref, other_ref, out_ref):
    gain = two_parts(own_ref[...] + other_ref[...]).astype(bf16)
    total = jnp.sum(pieces_ref[...].astype(f32), axis=0).astype(bf16)
    for part in range(2 * NL):
        out_ref[part, 0:64] = total[64 * part : 64 * part + 64]
        out_ref[part, 64:80] = gain


def next_sum_kernel(pieces_ref, out_ref):
    total = jnp.sum(pieces_ref[...].astype(f32), axis=0)
    gain = two_parts(total[64:72] + total[72:80])
    block = jnp.concatenate([total[0:64], gain], axis=0).astype(bf16)
    for copy in range(out_ref.shape[0]):
        out_ref[copy] = block


def finish_kernel(parts_ref, out_ref, gain_ref, left, right):
    gain = jnp.zeros((8, 128), f32)
    for x in range(NX):
        both = parts_ref[NL * x, 64:80].astype(f32)
        gain = gain + both[0:8] + both[8:16]
    gain_ref[...] = jnp.concatenate([gain[0:1], gain[1:2, 0:64]], axis=1)
    rows = parts_ref[:, 0:64].astype(f32).reshape(1024, 128)
    low = jnp.concatenate([rows[512:768], rows[928:1008]], axis=0)
    left[0:512] = rows[0:512]
    left[512:672] = rows[768:928]
    right[0:336] = low
    right[336:672] = pltpu.roll(low, 64, axis=1)
    for tap in range(27):
        even, odd = pl.ds(24 * tap, 12, stride=2), pl.ds(24 * tap + 1, 12, stride=2)
        tiles = [left[even, :], right[even, :][:, :64], left[odd, :], right[odd, :][:, :64]]
        out_ref[tap] = jnp.concatenate(tiles, axis=1)


SPECS = {"s": pltpu.SMEM, "v": pltpu.VMEM}


def call(kernel, name, places, operands, out_shapes, scratch=()):
    return pl.pallas_call(
        kernel,
        name=name,
        out_shape=out_shapes,
        in_specs=[pl.BlockSpec(memory_space=SPECS[place]) for place in places],
        out_specs=jax.tree.map(lambda unused: pl.BlockSpec(memory_space=pltpu.VMEM), out_shapes),
        scratch_shapes=list(scratch),
        compiler_params=pltpu.CompilerParams(vmem_limit_bytes=VMEM_LIMIT),
    )(*operands)


def to_next(by):
    return [(lane, (lane + by) % LANES) for lane in range(LANES)]


def on_device(video_latents, cotangent, conv_weight, norm_gain, clip_lengths):
    shape = jax.ShapeDtypeStruct
    ring = ("x", "zh", "zl")
    latent = video_latents[0, :, 0]
    upstream_raw = cotangent[0, :, 0]
    gain = norm_gain.reshape(1, C)
    lane = (lax.axis_index("x") * NH + lax.axis_index("zh")) * NL + lax.axis_index("zl")
    place = jnp.stack([lane, lax.axis_index("core")]).astype(jnp.int32)
    numbers = jnp.concatenate([clip_lengths[0], place])
    swap = [(0, 1), (1, 0)]

    share = call(
        share_kernel, "share", "v", (conv_weight.reshape(27, 12, 2 * C),),
        shape((NY, 336, 2 * C), bf16), [pltpu.VMEM((336, 2 * C), f32)],
    )
    latest, share = lax.optimization_barrier((latent, share))
    own = lax.all_to_all(share, ("yh", "yl"), 0, 0, tiled=True)
    after = lax.ppermute(upstream_raw[:, :2], ring, to_next(-1))
    before = lax.ppermute(latest[:, 2:], ring, to_next(1))
    both = call(
        prepare_kernel, "prepare", "svvv", (numbers, latest, upstream_raw, gain),
        shape((768, C), bf16),
    )
    both = call(
        pack_kernel, "pack", "svvvv", (numbers, both, before, after, gain), shape((1024, C), bf16)
    )
    other_both = lax.ppermute(both, "core", swap)
    pieces = pl.pallas_call(
        weight_kernel,
        name="weight_grad",
        out_shape=shape((NX, 2, 2, 256, 128), bf16),
        in_specs=[pl.BlockSpec(memory_space=SPECS[place]) for place in "svv"],
        out_specs=pl.BlockSpec(memory_space=pltpu.HBM),
        scratch_shapes=[
            pltpu.VMEM((2, 3, 6, 6, 16, 256), bf16), pltpu.VMEM((NY, 672, 256), f32),
            pltpu.VMEM((NX, NY, 256, 128), bf16), pltpu.SemaphoreType.DMA((NX * NY,)),
        ],
        compiler_params=pltpu.CompilerParams(vmem_limit_bytes=VMEM_LIMIT),
    )(place, both, other_both)
    pieces, own = lax.optimization_barrier((pieces, own))
    pieces = lax.all_to_all(pieces.reshape(NX * 2, 512, 128), ("x", "yl"), 0, 0, tiled=True)

    part = shape((256, 128), f32)
    own_grad, other_grad, gain_part = call(
        adjoint_kernel, "adjoint", "svvvv", (place, both, other_both, own, gain),
        (part, part, shape((8, 128), f32)),
        [pltpu.VMEM((2, 3, 6, 6, 16, C), bf16), pltpu.VMEM((NY, 336, 2 * C), f32)],
    )
    gain_other = lax.ppermute(gain_part, "core", swap)
    pair = call(add_kernel, "gain_pair", "vv", (gain_part, gain_other), shape((8, 128), f32))
    near = lax.ppermute(pair, "yl", swap)
    mixed, back = call(
        forward_kernel, "forward", "svvvv", (place, both, other_both, own, other_grad),
        (shape((256, C), f32), shape((256, 2 * C), f32)),
        [pltpu.VMEM((2, 3, 6, 6, 16, 128), bf16), pltpu.VMEM((NY, 336, 2 * C), f32)],
    )
    pieces, back = lax.optimization_barrier((pieces, back))
    blocks = call(
        first_sum_kernel, "first_sum", "vvv", (pieces, pair, near),
        shape((2 * NL, 80, 128), bf16),
    )
    blocks = lax.all_to_all(blocks, ("yh", "zl"), 0, 0, tiled=True)
    blocks = call(next_sum_kernel, "second_sum", "v", (blocks,), shape((NH, 80, 128), bf16))
    blocks = lax.all_to_all(blocks, "zh", 0, 0, tiled=True)
    back = lax.ppermute(back, "core", swap)
    decoded, latent_grad = call(
        output_kernel, "outputs", "svvvvv", (place, both, own_grad, mixed, back, gain),
        (shape(latent.shape, bf16),) * 2,
    )

    blocks = call(next_sum_kernel, "third_sum", "v", (blocks,), shape((NX * NL, 80, 128), bf16))
    blocks = lax.all_to_all(blocks, ("x", "zl"), 0, 0, tiled=True)
    weight_grad, gain_grad = call(
        finish_kernel, "finish", "v", (blocks,),
        (shape((27, 12, 2 * C), f32), shape((1, C), f32)), [pltpu.VMEM((672, 128), f32)] * 2,
    )
    return (
        decoded[None, :, None],
        latent_grad[None, :, None],
        weight_grad.reshape(3, 3, 3, 12, 2 * C),
        gain_grad.reshape(C),
    )


def solution(mesh):
    names = ("x", "zh", "zl", "yh", "yl", "core")
    axes = Mesh(mesh.devices.reshape(NX, NH, NL, 2, 2, NCORE), names)
    dp, clip = ("yh", "yl", "core"), ("x", "zh", "zl")
    data = P(dp, None, clip, None, None, None)
    kernel = P(None, None, None, dp, None)
    return jax.shard_map(
        on_device,
        mesh=axes,
        in_specs=(data, data, kernel, P(), P(dp, None)),
        out_specs=(data, data, kernel, P()),
        check_vma=False,
    )
```

```python
import jax
import jax.numpy as jnp
from jax import lax
from jax.experimental import pallas as pl
from jax.experimental.pallas import tpu as pltpu
from jax.sharding import Mesh, PartitionSpec as P

epsilon = 1e-06
bf16 = jnp.bfloat16
f32 = jnp.float32
C = 192
NX, NH, NL, NY, NCORE = 4, 4, 4, 4, 2
LANES = NX * NH * NL
VMEM_LIMIT = 24 * 1024 * 1024


def scalars(numbers_ref):
    count = numbers_ref.shape[0] - 2
    lane = numbers_ref[count]
    infos = []
    for wave in range(2):
        q = wave * LANES + lane
        begin = jnp.int32(0)
        length = jnp.int32(0)
        starts = jnp.int32(0)
        next_starts = jnp.int32(0)
        for k in range(count):
            own = numbers_ref[k]
            end = begin + own
            inside = jnp.logical_and(q >= begin, q < end)
            length = length + jnp.where(inside, own, 0)
            starts = starts + jnp.where(q == begin, 1, 0)
            next_starts = next_starts + jnp.where(q + 1 == begin, 1, 0)
            begin = end
        same = jnp.where(starts == 0, 1, 0)
        following = jnp.where(
            jnp.logical_and(next_starts == 0, q + 1 < 2 * LANES), 1, 0
        )
        infos.append((length, same, following))
    return lane, numbers_ref[count + 1], infos


def per_row(first, second):
    row = lax.broadcasted_iota(jnp.int32, (16, 1), 0)
    return jnp.where(row < 8, first.astype(f32), second.astype(f32))


def cells(block, frames):
    values = block.astype(f32)
    parts = []
    for frame in range(frames):
        for column in range(4):
            for wave in range(2):
                parts.append(values[wave, frame, :, column * C : (column + 1) * C])
    return jnp.concatenate(parts, axis=0)


def store_cells(ref, values):
    for frame in range(4):
        for wave in range(2):
            tiles = []
            for column in range(4):
                start = (frame * 4 + column) * 16 + wave * 8
                tiles.append(values[start : start + 8, :])
            ref[wave, frame] = jnp.concatenate(tiles, axis=1).astype(ref.dtype)


def times_rows(values, rows):
    n = values.shape[0] // 16
    return (values.reshape(n, 16, values.shape[1]) * rows[None]).reshape(values.shape)


def activate(values, gain):
    scale = lax.rsqrt(jnp.sum(values * values, axis=-1, keepdims=True) * (1.0 / C) + epsilon)
    normed = values * scale
    act = normed * gain
    sigma = 1.0 / (1.0 + jnp.exp(-act))
    return scale, normed, act, sigma


def store_shifted(padded, values):
    rows, width = values.shape
    frames = rows // 64
    at = lax.broadcasted_iota(jnp.int32, (rows, 1), 0) % 8
    zero = jnp.zeros((frames, 16, width), bf16)
    for shift in range(3):
        if shift == 0:
            moved = jnp.where(at == 0, 0.0, pltpu.roll(values, 1, axis=0))
        elif shift == 1:
            moved = values
        else:
            moved = jnp.where(at == 7, 0.0, pltpu.roll(values, rows - 1, axis=0))
        padded[shift, :, 0] = zero
        padded[shift, :, 5] = zero
        padded[shift, :, 1:5] = moved.astype(bf16).reshape(frames, 4, 16, width)


def wave_before(block, lane):
    first, second = block[0].astype(f32), block[1].astype(f32)
    return jnp.stack([first, jnp.where(lane == 0, first, second)], axis=0)


def wave_after(block, lane):
    first, second = block[0].astype(f32), block[1].astype(f32)
    return jnp.stack([jnp.where(lane == LANES - 1, second, first), second], axis=0)


def prepare_kernel(numbers_ref, latent_ref, cotangent_ref, gain_ref, both_ref):
    lane, core, infos = scalars(numbers_ref)
    weight = 1.0 / per_row(infos[0][0], infos[1][0])
    latent = cells(latent_ref[...], 4)
    unused, unused, act, sigma = activate(latent, gain_ref[...])
    both_ref[0:256] = (act * sigma).astype(bf16)
    both_ref[256:512] = times_rows(cells(cotangent_ref[...], 4), weight).astype(bf16)
    both_ref[512:768] = latent.astype(bf16)


def pack_kernel(numbers_ref, both_ref, before_ref, after_ref, gain_ref, out_ref):
    lane, core, infos = scalars(numbers_ref)
    weight = 1.0 / per_row(infos[0][0], infos[1][0])
    same = per_row(infos[0][1], infos[1][1])
    following = per_row(infos[0][2], infos[1][2])
    out_ref[0:768] = both_ref[...]
    unused, unused, act, sigma = activate(cells(wave_before(before_ref, lane), 2), gain_ref[...])
    out_ref[768:896] = times_rows(act * sigma, same).astype(bf16)
    after = times_rows(cells(wave_after(after_ref, lane), 2), weight)
    out_ref[896:1024] = times_rows(after, following).astype(bf16)


def selection(core):
    channel = lax.broadcasted_iota(jnp.int32, (C, 128), 0)
    place = lax.broadcasted_iota(jnp.int32, (C, 128), 1)
    hit = jnp.logical_and(channel == 24 * (2 * (place // 24) + core) + place % 24, place < 96)
    return jnp.where(hit, 1.0, 0.0).astype(bf16)


def weight_kernel(place_ref, own_ref, other_ref, out_hbm, wide, grads, out_ref, semaphores):
    core = place_ref[1]
    select = selection(core)
    hidden = []
    for r, block in enumerate((own_ref, other_ref)):
        hidden.append(jnp.dot(block[0:256], select, preferred_element_type=f32))
        upstream = jnp.concatenate([block[256:512], block[896:1024]], axis=0).astype(f32)
        blank = jnp.zeros((384, 64), f32)
        store_shifted(wide.at[r], jnp.concatenate([upstream, blank], axis=1))
    hidden = jnp.transpose(jnp.concatenate(hidden, axis=0)).astype(bf16)
    copies = []

    def send(x):
        for y in range(NY):
            target = out_hbm.at[x, y % 2, y // 2]
            copy = pltpu.make_async_copy(out_ref.at[x, y], target, semaphores.at[NY * x + y])
            copy.start()
            copies.append(copy)

    def high_half(y, start, stop):
        early = grads[y, start:stop, 128:256]
        return (early + grads[y, 336 + start : 336 + stop, 128:256]).astype(bf16)

    for tap in range(27):
        t, i, j = tap // 9, (tap // 3) % 3, tap % 3
        patch = [
            wide[r, 2 - i, 2 - t : 6 - t, 2 - j : 6 - j].reshape(256, 256) for r in range(2)
        ]
        part = jnp.dot(hidden, jnp.concatenate(patch, axis=0), preferred_element_type=f32)[:96]
        rows = slice(24 * tap, 24 * tap + 24)
        grads[:, rows, 0:128] = part[:, :128].reshape(NY, 24, 128)
        high = part[:, 128:] if tap < 14 else pltpu.roll(part[:, 128:], 64, axis=1)
        grads[:, rows, 128:256] = high.reshape(NY, 24, 128)
        if tap == 10 or tap == 21:
            x = tap // 20
            for y in range(NY):
                out_ref[x, y] = grads[y, 256 * x : 256 * x + 256, 0:128].astype(bf16)
            send(x)
        if tap == 24:
            for y in range(NY):
                out_ref[2, y] = high_half(y, 0, 256)
            send(2)
    grads[:, 648:672, :] = jnp.zeros((NY, 24, 256), f32)
    for y in range(NY):
        out_ref[3, y, 0:160] = grads[y, 512:672, 0:128].astype(bf16)
        out_ref[3, y, 160:240] = high_half(y, 256, 336)
        out_ref[3, y, 240:256] = jnp.zeros((16, 128), bf16)
    send(3)
    for copy in copies:
        copy.wait()


def share_kernel(share_ref, out_ref, flat):
    for tap in range(27):
        flat[12 * tap : 12 * tap + 12, :] = share_ref[tap].astype(f32)
    flat[324:336, :] = jnp.zeros((12, 2 * C), f32)
    block = flat[...].astype(bf16)
    for y in range(NY):
        out_ref[y] = block


def permutation(core):
    channel = lax.broadcasted_iota(jnp.int32, (C, 128), 0)
    place = lax.broadcasted_iota(jnp.int32, (C, 128), 1)
    h, y, r = place // 64, (place % 64) // 16, place % 16
    hit = jnp.logical_and(channel == 24 * (2 * y + core) + 2 * r + h, r < 12)
    return jnp.where(hit, 1.0, 0.0).astype(bf16)


def split_dot(values, matrix, dimensions, parts=3):
    total = 0.0
    for unused in range(parts):
        part = values.astype(bf16)
        values = values - part.astype(f32)
        total = total + lax.dot_general(part, matrix, dimensions, preferred_element_type=f32)
    return total


FORTH = (((1,), (0,)), ((), ()))
BACK = (((1,), (1,)), ((), ()))


def unpack(shares_ref, rows_ref):
    for y in range(NY):
        rows_ref[y] = shares_ref[y].astype(f32)


def tap_matrix(rows_ref, tap):
    parts = [rows_ref[y, 12 * tap : 12 * tap + 16, :].astype(bf16) for y in range(NY)]
    rows = jnp.concatenate(parts, axis=0)
    return jnp.concatenate([rows[:, :C], rows[:, C:]], axis=0)


def adjoint_kernel(
    place_ref, own_ref, other_ref, shares_ref, gain_ref,
    own_grad_ref, other_grad_ref, gain_part_ref, wide, rows_ref,
):
    core = place_ref[1]
    unpack(shares_ref, rows_ref)
    order = permutation(core)
    factors = []
    for r, block in enumerate((own_ref, other_ref)):
        upstream = jnp.concatenate([block[256:512], block[896:1024]], axis=0).astype(f32)
        store_shifted(wide.at[r], upstream)
        unused, normed, act, sigma = activate(block[512:768].astype(f32), gain_ref[...])
        factors.append(sigma * (1.0 + act * (1.0 - sigma)) * normed)
    factors = split_dot(jnp.concatenate(factors, axis=0), order, FORTH)
    hidden_grad = jnp.zeros((512, 128), f32)
    for tap in range(27):
        t, i, j = tap // 9, (tap // 3) % 3, tap % 3
        patch = [
            wide[r, 2 - i, 2 - t : 6 - t, 2 - j : 6 - j].reshape(256, C) for r in range(2)
        ]
        hidden_grad = hidden_grad + lax.dot_general(
            jnp.concatenate(patch, axis=0), tap_matrix(rows_ref, tap), BACK,
            preferred_element_type=f32,
        )
    own_grad_ref[...] = hidden_grad[:256]
    other_grad_ref[...] = hidden_grad[256:]
    gain_part = jnp.sum(hidden_grad * factors, axis=0, keepdims=True)
    gain_part = split_dot(gain_part, order, BACK)
    gain_part_ref[...] = jnp.zeros((8, 128), f32)
    gain_part_ref[0:1, :] = gain_part[:, :128]
    gain_part_ref[1:2, 0:64] = gain_part[:, 128:]


def forward_kernel(
    place_ref, own_ref, other_ref, shares_ref, own_grad_ref, other_grad_ref,
    mixed_ref, back_ref, padded, rows_ref,
):
    core = place_ref[1]
    unpack(shares_ref, rows_ref)
    order = permutation(core)
    for r, block in enumerate((own_ref, other_ref)):
        hidden = jnp.concatenate([block[768:896], block[0:256]], axis=0)
        store_shifted(padded.at[r], jnp.dot(hidden, order, preferred_element_type=f32))
    mixed = jnp.zeros((512, C), f32)
    for tap in range(27):
        t, i, j = tap // 9, (tap // 3) % 3, tap % 3
        patch = [padded[r, i, t : t + 4, j : j + 4].reshape(256, 128) for r in range(2)]
        mixed = mixed + jnp.dot(
            jnp.concatenate(patch, axis=0), tap_matrix(rows_ref, tap), preferred_element_type=f32
        )
    mixed_ref[0:256] = mixed[:256]
    mixed_ref[256:512] = split_dot(own_grad_ref[...], order, BACK, 2)
    back_ref[:, 0:128] = other_grad_ref[...]
    back_ref[:, 128:320] = mixed[256:]
    back_ref[:, 320:384] = jnp.zeros((256, 64), f32)


def output_kernel(
    place_ref, both_ref, mixed_ref, back_ref, gain_ref, decoded_ref, latent_grad_ref
):
    core = place_ref[1]
    latent = both_ref[512:768].astype(f32)
    store_cells(decoded_ref, latent + (mixed_ref[0:256] + back_ref[:, 128:320]))
    hidden_grad = mixed_ref[256:512] + split_dot(
        back_ref[:, 0:128], permutation(1 - core), BACK, 2
    )
    gain = gain_ref[...]
    scale, normed, act, sigma = activate(latent, gain)
    inner = hidden_grad * sigma * (1.0 + act * (1.0 - sigma)) * gain
    mean = jnp.sum(inner * normed, axis=-1, keepdims=True) * (1.0 / C)
    upstream = both_ref[256:512].astype(f32)
    store_cells(latent_grad_ref, upstream + scale * (inner - normed * mean))


def two_parts(gain):
    coarse = gain.astype(bf16).astype(f32)
    return jnp.concatenate([coarse, gain - coarse], axis=0)


def add_kernel(own_ref, other_ref, out_ref):
    out_ref[...] = own_ref[...] + other_ref[...]


def first_sum_kernel(pieces_ref, own_ref, other_ref, out_ref):
    gain = two_parts(own_ref[...] + other_ref[...]).astype(bf16)
    total = jnp.sum(pieces_ref[...].astype(f32), axis=0).astype(bf16)
    for part in range(2 * NL):
        out_ref[part, 0:64] = total[64 * part : 64 * part + 64]
        out_ref[part, 64:80] = gain


def next_sum_kernel(pieces_ref, out_ref):
    total = jnp.sum(pieces_ref[...].astype(f32), axis=0)
    gain = two_parts(total[64:72] + total[72:80])
    block = jnp.concatenate([total[0:64], gain], axis=0).astype(bf16)
    for copy in range(out_ref.shape[0]):
        out_ref[copy] = block


def finish_kernel(parts_ref, out_ref, gain_ref, left, right):
    gain = jnp.zeros((8, 128), f32)
    for x in range(NX):
        both = parts_ref[NL * x, 64:80].astype(f32)
        gain = gain + both[0:8] + both[8:16]
    gain_ref[...] = jnp.concatenate([gain[0:1], gain[1:2, 0:64]], axis=1)
    rows = parts_ref[:, 0:64].astype(f32).reshape(1024, 128)
    low = jnp.concatenate([rows[512:768], rows[928:1008]], axis=0)
    left[0:512] = rows[0:512]
    left[512:672] = rows[768:928]
    right[0:336] = low
    right[336:672] = pltpu.roll(low, 64, axis=1)
    for tap in range(27):
        even, odd = pl.ds(24 * tap, 12, stride=2), pl.ds(24 * tap + 1, 12, stride=2)
        tiles = [left[even, :], right[even, :][:, :64], left[odd, :], right[odd, :][:, :64]]
        out_ref[tap] = jnp.concatenate(tiles, axis=1)


SPECS = {"s": pltpu.SMEM, "v": pltpu.VMEM}


def call(kernel, name, places, operands, out_shapes, scratch=()):
    return pl.pallas_call(
        kernel,
        name=name,
        out_shape=out_shapes,
        in_specs=[pl.BlockSpec(memory_space=SPECS[place]) for place in places],
        out_specs=jax.tree.map(lambda unused: pl.BlockSpec(memory_space=pltpu.VMEM), out_shapes),
        scratch_shapes=list(scratch),
        compiler_params=pltpu.CompilerParams(vmem_limit_bytes=VMEM_LIMIT),
    )(*operands)


def to_next(by):
    return [(lane, (lane + by) % LANES) for lane in range(LANES)]


def on_device(video_latents, cotangent, conv_weight, norm_gain, clip_lengths):
    shape = jax.ShapeDtypeStruct
    ring = ("x", "zh", "zl")
    latent = video_latents[0, :, 0]
    upstream_raw = cotangent[0, :, 0]
    gain = norm_gain.reshape(1, C)
    lane = (lax.axis_index("x") * NH + lax.axis_index("zh")) * NL + lax.axis_index("zl")
    place = jnp.stack([lane, lax.axis_index("core")]).astype(jnp.int32)
    numbers = jnp.concatenate([clip_lengths[0], place])
    swap = [(0, 1), (1, 0)]

    share = call(
        share_kernel, "share", "v", (conv_weight.reshape(27, 12, 2 * C),),
        shape((NY, 336, 2 * C), bf16), [pltpu.VMEM((336, 2 * C), f32)],
    )
    latest, share = lax.optimization_barrier((latent, share))
    own = lax.all_to_all(share, ("yh", "yl"), 0, 0, tiled=True)
    after = lax.ppermute(upstream_raw[:, :2], ring, to_next(-1))
    before = lax.ppermute(latest[:, 2:], ring, to_next(1))
    both = call(
        prepare_kernel, "prepare", "svvv", (numbers, latest, upstream_raw, gain),
        shape((768, C), bf16),
    )
    both = call(
        pack_kernel, "pack", "svvvv", (numbers, both, before, after, gain), shape((1024, C), bf16)
    )
    other_both = lax.ppermute(both, "core", swap)
    pieces = pl.pallas_call(
        weight_kernel,
        name="weight_grad",
        out_shape=shape((NX, 2, 2, 256, 128), bf16),
        in_specs=[pl.BlockSpec(memory_space=SPECS[place]) for place in "svv"],
        out_specs=pl.BlockSpec(memory_space=pltpu.HBM),
        scratch_shapes=[
            pltpu.VMEM((2, 3, 6, 6, 16, 256), bf16), pltpu.VMEM((NY, 672, 256), f32),
            pltpu.VMEM((NX, NY, 256, 128), bf16), pltpu.SemaphoreType.DMA((NX * NY,)),
        ],
        compiler_params=pltpu.CompilerParams(vmem_limit_bytes=VMEM_LIMIT),
    )(place, both, other_both)
    pieces, own = lax.optimization_barrier((pieces, own))
    pieces = lax.all_to_all(pieces.reshape(NX * 2, 512, 128), ("x", "yl"), 0, 0, tiled=True)

    part = shape((256, 128), f32)
    own_grad, other_grad, gain_part = call(
        adjoint_kernel, "adjoint", "svvvv", (place, both, other_both, own, gain),
        (part, part, shape((8, 128), f32)),
        [pltpu.VMEM((2, 3, 6, 6, 16, C), bf16), pltpu.VMEM((NY, 336, 2 * C), f32)],
    )
    gain_other = lax.ppermute(gain_part, "core", swap)
    pair = call(add_kernel, "gain_pair", "vv", (gain_part, gain_other), shape((8, 128), f32))
    near = lax.ppermute(pair, "yl", swap)
    mixed, back = call(
        forward_kernel, "forward", "svvvvv", (place, both, other_both, own, own_grad, other_grad),
        (shape((512, C), f32), shape((256, 2 * C), f32)),
        [pltpu.VMEM((2, 3, 6, 6, 16, 128), bf16), pltpu.VMEM((NY, 336, 2 * C), f32)],
    )
    pieces, back = lax.optimization_barrier((pieces, back))
    blocks = call(
        first_sum_kernel, "first_sum", "vvv", (pieces, pair, near),
        shape((2 * NL, 80, 128), bf16),
    )
    blocks = lax.all_to_all(blocks, ("yh", "zl"), 0, 0, tiled=True)
    blocks = call(next_sum_kernel, "second_sum", "v", (blocks,), shape((NH, 80, 128), bf16))
    blocks = lax.all_to_all(blocks, "zh", 0, 0, tiled=True)
    back = lax.ppermute(back, "core", swap)
    decoded, latent_grad = call(
        output_kernel, "outputs", "svvvv", (place, both, mixed, back, gain),
        (shape(latent.shape, bf16),) * 2,
    )

    blocks = call(next_sum_kernel, "third_sum", "v", (blocks,), shape((NX * NL, 80, 128), bf16))
    blocks = lax.all_to_all(blocks, ("x", "zl"), 0, 0, tiled=True)
    weight_grad, gain_grad = call(
        finish_kernel, "finish", "v", (blocks,),
        (shape((27, 12, 2 * C), f32), shape((1, C), f32)), [pltpu.VMEM((672, 128), f32)] * 2,
    )
    return (
        decoded[None, :, None],
        latent_grad[None, :, None],
        weight_grad.reshape(3, 3, 3, 12, 2 * C),
        gain_grad.reshape(C),
    )


def solution(mesh):
    names = ("x", "zh", "zl", "yh", "yl", "core")
    axes = Mesh(mesh.devices.reshape(NX, NH, NL, 2, 2, NCORE), names)
    dp, clip = ("yh", "yl", "core"), ("x", "zh", "zl")
    data = P(dp, None, clip, None, None, None)
    kernel = P(None, None, None, dp, None)
    return jax.shard_map(
        on_device,
        mesh=axes,
        in_specs=(data, data, kernel, P(), P(dp, None)),
        out_specs=(data, data, kernel, P()),
        check_vma=False,
    )
```

```python
import jax
import jax.numpy as jnp
from jax import lax
from jax.experimental import pallas as pl
from jax.experimental.pallas import tpu as pltpu
from jax.sharding import Mesh, PartitionSpec as P

epsilon = 1e-06
bf16 = jnp.bfloat16
f32 = jnp.float32
C = 192
NX, NH, NL, NY, NCORE = 4, 4, 4, 4, 2
LANES = NX * NH * NL
VMEM_LIMIT = 24 * 1024 * 1024


def scalars(numbers_ref):
    count = numbers_ref.shape[0] - 2
    lane = numbers_ref[count]
    infos = []
    for wave in range(2):
        q = wave * LANES + lane
        begin = jnp.int32(0)
        length = jnp.int32(0)
        starts = jnp.int32(0)
        next_starts = jnp.int32(0)
        for k in range(count):
            own = numbers_ref[k]
            end = begin + own
            inside = jnp.logical_and(q >= begin, q < end)
            length = length + jnp.where(inside, own, 0)
            starts = starts + jnp.where(q == begin, 1, 0)
            next_starts = next_starts + jnp.where(q + 1 == begin, 1, 0)
            begin = end
        same = jnp.where(starts == 0, 1, 0)
        following = jnp.where(
            jnp.logical_and(next_starts == 0, q + 1 < 2 * LANES), 1, 0
        )
        infos.append((length, same, following))
    return lane, numbers_ref[count + 1], infos


def per_row(first, second):
    row = lax.broadcasted_iota(jnp.int32, (16, 1), 0)
    return jnp.where(row < 8, first.astype(f32), second.astype(f32))


def cells(block, frames):
    values = block.astype(f32)
    parts = []
    for frame in range(frames):
        for column in range(4):
            for wave in range(2):
                parts.append(values[wave, frame, :, column * C : (column + 1) * C])
    return jnp.concatenate(parts, axis=0)


def store_cells(ref, values):
    for frame in range(4):
        for wave in range(2):
            tiles = []
            for column in range(4):
                start = (frame * 4 + column) * 16 + wave * 8
                tiles.append(values[start : start + 8, :])
            ref[wave, frame] = jnp.concatenate(tiles, axis=1).astype(ref.dtype)


def times_rows(values, rows):
    n = values.shape[0] // 16
    return (values.reshape(n, 16, values.shape[1]) * rows[None]).reshape(values.shape)


def activate(values, gain):
    scale = lax.rsqrt(jnp.sum(values * values, axis=-1, keepdims=True) * (1.0 / C) + epsilon)
    normed = values * scale
    act = normed * gain
    sigma = 1.0 / (1.0 + jnp.exp(-act))
    return scale, normed, act, sigma


def store_shifted(padded, values):
    rows, width = values.shape
    frames = rows // 64
    at = lax.broadcasted_iota(jnp.int32, (rows, 1), 0) % 8
    zero = jnp.zeros((frames, 16, width), bf16)
    for shift in range(3):
        if shift == 0:
            moved = jnp.where(at == 0, 0.0, pltpu.roll(values, 1, axis=0))
        elif shift == 1:
            moved = values
        else:
            moved = jnp.where(at == 7, 0.0, pltpu.roll(values, rows - 1, axis=0))
        padded[shift, :, 0] = zero
        padded[shift, :, 5] = zero
        padded[shift, :, 1:5] = moved.astype(bf16).reshape(frames, 4, 16, width)


def wave_before(block, lane):
    first, second = block[0].astype(f32), block[1].astype(f32)
    return jnp.stack([first, jnp.where(lane == 0, first, second)], axis=0)


def wave_after(block, lane):
    first, second = block[0].astype(f32), block[1].astype(f32)
    return jnp.stack([jnp.where(lane == LANES - 1, second, first), second], axis=0)


def prepare_kernel(numbers_ref, latent_ref, cotangent_ref, gain_ref, both_ref):
    lane, core, infos = scalars(numbers_ref)
    weight = 1.0 / per_row(infos[0][0], infos[1][0])
    latent = cells(latent_ref[...], 4)
    unused, unused, act, sigma = activate(latent, gain_ref[...])
    both_ref[0:256] = (act * sigma).astype(bf16)
    both_ref[256:512] = times_rows(cells(cotangent_ref[...], 4), weight).astype(bf16)
    both_ref[512:768] = latent.astype(bf16)


def pack_kernel(numbers_ref, both_ref, before_ref, after_ref, gain_ref, out_ref):
    lane, core, infos = scalars(numbers_ref)
    weight = 1.0 / per_row(infos[0][0], infos[1][0])
    same = per_row(infos[0][1], infos[1][1])
    following = per_row(infos[0][2], infos[1][2])
    unused, unused, act, sigma = activate(cells(wave_before(before_ref, lane), 2), gain_ref[...])
    out_ref[768:896] = times_rows(act * sigma, same).astype(bf16)
    after = times_rows(cells(wave_after(after_ref, lane), 2), weight)
    out_ref[896:1024] = times_rows(after, following).astype(bf16)


def selection(core):
    channel = lax.broadcasted_iota(jnp.int32, (C, 128), 0)
    place = lax.broadcasted_iota(jnp.int32, (C, 128), 1)
    hit = jnp.logical_and(channel == 24 * (2 * (place // 24) + core) + place % 24, place < 96)
    return jnp.where(hit, 1.0, 0.0).astype(bf16)


def weight_kernel(place_ref, own_ref, other_ref, out_hbm, wide, grads, out_ref, semaphores):
    core = place_ref[1]
    select = selection(core)
    hidden = []
    for r, block in enumerate((own_ref, other_ref)):
        hidden.append(jnp.dot(block[0:256], select, preferred_element_type=f32))
        upstream = jnp.concatenate([block[256:512], block[896:1024]], axis=0).astype(f32)
        blank = jnp.zeros((384, 64), f32)
        store_shifted(wide.at[r], jnp.concatenate([upstream, blank], axis=1))
    hidden = jnp.transpose(jnp.concatenate(hidden, axis=0)).astype(bf16)
    copies = []

    def send(x):
        for y in range(NY):
            target = out_hbm.at[x, y % 2, y // 2]
            copy = pltpu.make_async_copy(out_ref.at[x, y], target, semaphores.at[NY * x + y])
            copy.start()
            copies.append(copy)

    def high_half(y, start, stop):
        early = grads[y, start:stop, 128:256]
        return (early + grads[y, 336 + start : 336 + stop, 128:256]).astype(bf16)

    for tap in range(27):
        t, i, j = tap // 9, (tap // 3) % 3, tap % 3
        patch = [
            wide[r, 2 - i, 2 - t : 6 - t, 2 - j : 6 - j].reshape(256, 256) for r in range(2)
        ]
        part = jnp.dot(hidden, jnp.concatenate(patch, axis=0), preferred_element_type=f32)[:96]
        rows = slice(24 * tap, 24 * tap + 24)
        grads[:, rows, 0:128] = part[:, :128].reshape(NY, 24, 128)
        high = part[:, 128:] if tap < 14 else pltpu.roll(part[:, 128:], 64, axis=1)
        grads[:, rows, 128:256] = high.reshape(NY, 24, 128)
        if tap == 10 or tap == 21:
            x = tap // 20
            for y in range(NY):
                out_ref[x, y] = grads[y, 256 * x : 256 * x + 256, 0:128].astype(bf16)
            send(x)
        if tap == 24:
            for y in range(NY):
                out_ref[2, y] = high_half(y, 0, 256)
            send(2)
    grads[:, 648:672, :] = jnp.zeros((NY, 24, 256), f32)
    for y in range(NY):
        out_ref[3, y, 0:160] = grads[y, 512:672, 0:128].astype(bf16)
        out_ref[3, y, 160:240] = high_half(y, 256, 336)
        out_ref[3, y, 240:256] = jnp.zeros((16, 128), bf16)
    send(3)
    for copy in copies:
        copy.wait()


def share_kernel(share_ref, out_ref, flat):
    for tap in range(27):
        flat[12 * tap : 12 * tap + 12, :] = share_ref[tap].astype(f32)
    flat[324:336, :] = jnp.zeros((12, 2 * C), f32)
    block = flat[...].astype(bf16)
    for y in range(NY):
        out_ref[y] = block


def permutation(core):
    channel = lax.broadcasted_iota(jnp.int32, (C, 128), 0)
    place = lax.broadcasted_iota(jnp.int32, (C, 128), 1)
    h, y, r = place // 64, (place % 64) // 16, place % 16
    hit = jnp.logical_and(channel == 24 * (2 * y + core) + 2 * r + h, r < 12)
    return jnp.where(hit, 1.0, 0.0).astype(bf16)


def split_dot(values, matrix, dimensions, parts=3):
    total = 0.0
    for unused in range(parts):
        part = values.astype(bf16)
        values = values - part.astype(f32)
        total = total + lax.dot_general(part, matrix, dimensions, preferred_element_type=f32)
    return total


FORTH = (((1,), (0,)), ((), ()))
BACK = (((1,), (1,)), ((), ()))


def unpack(shares_ref, rows_ref):
    for y in range(NY):
        rows_ref[y] = shares_ref[y].astype(f32)


def tap_matrix(rows_ref, tap):
    parts = [rows_ref[y, 12 * tap : 12 * tap + 16, :].astype(bf16) for y in range(NY)]
    rows = jnp.concatenate(parts, axis=0)
    return jnp.concatenate([rows[:, :C], rows[:, C:]], axis=0)


def adjoint_kernel(
    place_ref, own_ref, other_ref, shares_ref, gain_ref,
    own_grad_ref, other_grad_ref, gain_part_ref, wide, rows_ref,
):
    core = place_ref[1]
    unpack(shares_ref, rows_ref)
    order = permutation(core)
    factors = []
    for r, block in enumerate((own_ref, other_ref)):
        upstream = jnp.concatenate([block[256:512], block[896:1024]], axis=0).astype(f32)
        store_shifted(wide.at[r], upstream)
        unused, normed, act, sigma = activate(block[512:768].astype(f32), gain_ref[...])
        factors.append(sigma * (1.0 + act * (1.0 - sigma)) * normed)
    factors = split_dot(jnp.concatenate(factors, axis=0), order, FORTH, 2)
    hidden_grad = jnp.zeros((512, 128), f32)
    for tap in range(27):
        t, i, j = tap // 9, (tap // 3) % 3, tap % 3
        patch = [
            wide[r, 2 - i, 2 - t : 6 - t, 2 - j : 6 - j].reshape(256, C) for r in range(2)
        ]
        hidden_grad = hidden_grad + lax.dot_general(
            jnp.concatenate(patch, axis=0), tap_matrix(rows_ref, tap), BACK,
            preferred_element_type=f32,
        )
    own_grad_ref[...] = hidden_grad[:256]
    other_grad_ref[...] = hidden_grad[256:]
    gain_part = jnp.sum(hidden_grad * factors, axis=0, keepdims=True)
    gain_part = split_dot(gain_part, order, BACK)
    gain_part_ref[...] = jnp.zeros((8, 128), f32)
    gain_part_ref[0:1, :] = gain_part[:, :128]
    gain_part_ref[1:2, 0:64] = gain_part[:, 128:]


def forward_kernel(
    place_ref, own_ref, other_ref, shares_ref, own_grad_ref, other_grad_ref,
    mixed_ref, back_ref, padded, rows_ref,
):
    core = place_ref[1]
    unpack(shares_ref, rows_ref)
    order = permutation(core)
    for r, block in enumerate((own_ref, other_ref)):
        hidden = jnp.concatenate([block[768:896], block[0:256]], axis=0)
        store_shifted(padded.at[r], jnp.dot(hidden, order, preferred_element_type=f32))
    mixed = jnp.zeros((512, C), f32)
    for tap in range(27):
        t, i, j = tap // 9, (tap // 3) % 3, tap % 3
        patch = [padded[r, i, t : t + 4, j : j + 4].reshape(256, 128) for r in range(2)]
        mixed = mixed + jnp.dot(
            jnp.concatenate(patch, axis=0), tap_matrix(rows_ref, tap), preferred_element_type=f32
        )
    mixed_ref[0:256] = mixed[:256]
    mixed_ref[256:512] = split_dot(own_grad_ref[...], order, BACK, 2)
    back_ref[:, 0:128] = other_grad_ref[...]
    back_ref[:, 128:320] = mixed[256:]
    back_ref[:, 320:384] = jnp.zeros((256, 64), f32)


def output_kernel(
    place_ref, both_ref, mixed_ref, back_ref, gain_ref, decoded_ref, latent_grad_ref
):
    core = place_ref[1]
    latent = both_ref[512:768].astype(f32)
    store_cells(decoded_ref, latent + (mixed_ref[0:256] + back_ref[:, 128:320]))
    hidden_grad = mixed_ref[256:512] + split_dot(
        back_ref[:, 0:128], permutation(1 - core), BACK, 2
    )
    gain = gain_ref[...]
    scale, normed, act, sigma = activate(latent, gain)
    inner = hidden_grad * sigma * (1.0 + act * (1.0 - sigma)) * gain
    mean = jnp.sum(inner * normed, axis=-1, keepdims=True) * (1.0 / C)
    upstream = both_ref[256:512].astype(f32)
    store_cells(latent_grad_ref, upstream + scale * (inner - normed * mean))


def two_parts(gain):
    coarse = gain.astype(bf16).astype(f32)
    return jnp.concatenate([coarse, gain - coarse], axis=0)


def add_kernel(own_ref, other_ref, out_ref):
    out_ref[...] = own_ref[...] + other_ref[...]


def first_sum_kernel(pieces_ref, own_ref, other_ref, out_ref):
    gain = two_parts(own_ref[...] + other_ref[...]).astype(bf16)
    total = jnp.sum(pieces_ref[...].astype(f32), axis=0).astype(bf16)
    for part in range(2 * NL):
        out_ref[part, 0:64] = total[64 * part : 64 * part + 64]
        out_ref[part, 64:80] = gain


def next_sum_kernel(pieces_ref, out_ref):
    total = jnp.sum(pieces_ref[...].astype(f32), axis=0)
    gain = two_parts(total[64:72] + total[72:80])
    block = jnp.concatenate([total[0:64], gain], axis=0).astype(bf16)
    for copy in range(out_ref.shape[0]):
        out_ref[copy] = block


def finish_kernel(parts_ref, out_ref, gain_ref, left, right):
    gain = jnp.zeros((8, 128), f32)
    for x in range(NX):
        both = parts_ref[NL * x, 64:80].astype(f32)
        gain = gain + both[0:8] + both[8:16]
    gain_ref[...] = jnp.concatenate([gain[0:1], gain[1:2, 0:64]], axis=1)
    rows = parts_ref[:, 0:64].astype(f32).reshape(1024, 128)
    low = jnp.concatenate([rows[512:768], rows[928:1008]], axis=0)
    left[0:512] = rows[0:512]
    left[512:672] = rows[768:928]
    right[0:336] = low
    right[336:672] = pltpu.roll(low, 64, axis=1)
    for tap in range(27):
        even, odd = pl.ds(24 * tap, 12, stride=2), pl.ds(24 * tap + 1, 12, stride=2)
        tiles = [left[even, :], right[even, :][:, :64], left[odd, :], right[odd, :][:, :64]]
        out_ref[tap] = jnp.concatenate(tiles, axis=1)


SPECS = {"s": pltpu.SMEM, "v": pltpu.VMEM}


def call(kernel, name, places, operands, out_shapes, scratch=(), aliases={}):
    return pl.pallas_call(
        kernel,
        name=name,
        out_shape=out_shapes,
        in_specs=[pl.BlockSpec(memory_space=SPECS[place]) for place in places],
        out_specs=jax.tree.map(lambda unused: pl.BlockSpec(memory_space=pltpu.VMEM), out_shapes),
        scratch_shapes=list(scratch),
        input_output_aliases=aliases,
        compiler_params=pltpu.CompilerParams(vmem_limit_bytes=VMEM_LIMIT),
    )(*operands)


def to_next(by):
    return [(lane, (lane + by) % LANES) for lane in range(LANES)]


def on_device(video_latents, cotangent, conv_weight, norm_gain, clip_lengths):
    shape = jax.ShapeDtypeStruct
    ring = ("x", "zh", "zl")
    latent = video_latents[0, :, 0]
    upstream_raw = cotangent[0, :, 0]
    gain = norm_gain.reshape(1, C)
    lane = (lax.axis_index("x") * NH + lax.axis_index("zh")) * NL + lax.axis_index("zl")
    place = jnp.stack([lane, lax.axis_index("core")]).astype(jnp.int32)
    numbers = jnp.concatenate([clip_lengths[0], place])
    swap = [(0, 1), (1, 0)]

    share = call(
        share_kernel, "share", "v", (conv_weight.reshape(27, 12, 2 * C),),
        shape((NY, 336, 2 * C), bf16), [pltpu.VMEM((336, 2 * C), f32)],
    )
    latest, share = lax.optimization_barrier((latent, share))
    own = lax.all_to_all(share, ("yh", "yl"), 0, 0, tiled=True)
    after = lax.ppermute(upstream_raw[:, :2], ring, to_next(-1))
    before = lax.ppermute(latest[:, 2:], ring, to_next(1))
    both = call(
        prepare_kernel, "prepare", "svvv", (numbers, latest, upstream_raw, gain),
        shape((1024, C), bf16),
    )
    both = call(
        pack_kernel, "pack", "svvvv", (numbers, both, before, after, gain), shape((1024, C), bf16),
        aliases={1: 0},
    )
    other_both = lax.ppermute(both, "core", swap)
    pieces = pl.pallas_call(
        weight_kernel,
        name="weight_grad",
        out_shape=shape((NX, 2, 2, 256, 128), bf16),
        in_specs=[pl.BlockSpec(memory_space=SPECS[place]) for place in "svv"],
        out_specs=pl.BlockSpec(memory_space=pltpu.HBM),
        scratch_shapes=[
            pltpu.VMEM((2, 3, 6, 6, 16, 256), bf16), pltpu.VMEM((NY, 672, 256), f32),
            pltpu.VMEM((NX, NY, 256, 128), bf16), pltpu.SemaphoreType.DMA((NX * NY,)),
        ],
        compiler_params=pltpu.CompilerParams(vmem_limit_bytes=VMEM_LIMIT),
    )(place, both, other_both)
    pieces, own = lax.optimization_barrier((pieces, own))
    pieces = lax.all_to_all(pieces.reshape(NX * 2, 512, 128), ("x", "yl"), 0, 0, tiled=True)

    part = shape((256, 128), f32)
    own_grad, other_grad, gain_part = call(
        adjoint_kernel, "adjoint", "svvvv", (place, both, other_both, own, gain),
        (part, part, shape((8, 128), f32)),
        [pltpu.VMEM((2, 3, 6, 6, 16, C), bf16), pltpu.VMEM((NY, 336, 2 * C), f32)],
    )
    gain_other = lax.ppermute(gain_part, "core", swap)
    pair = call(add_kernel, "gain_pair", "vv", (gain_part, gain_other), shape((8, 128), f32))
    near = lax.ppermute(pair, "yl", swap)
    mixed, back = call(
        forward_kernel, "forward", "svvvvv", (place, both, other_both, own, own_grad, other_grad),
        (shape((512, C), f32), shape((256, 2 * C), f32)),
        [pltpu.VMEM((2, 3, 6, 6, 16, 128), bf16), pltpu.VMEM((NY, 336, 2 * C), f32)],
    )
    pieces, back = lax.optimization_barrier((pieces, back))
    blocks = call(
        first_sum_kernel, "first_sum", "vvv", (pieces, pair, near),
        shape((2 * NL, 80, 128), bf16),
    )
    blocks = lax.all_to_all(blocks, ("yh", "zl"), 0, 0, tiled=True)
    blocks = call(next_sum_kernel, "second_sum", "v", (blocks,), shape((NH, 80, 128), bf16))
    blocks = lax.all_to_all(blocks, "zh", 0, 0, tiled=True)
    back = lax.ppermute(back, "core", swap)
    decoded, latent_grad = call(
        output_kernel, "outputs", "svvvv", (place, both, mixed, back, gain),
        (shape(latent.shape, bf16),) * 2,
    )

    blocks = call(next_sum_kernel, "third_sum", "v", (blocks,), shape((NX * NL, 80, 128), bf16))
    blocks = lax.all_to_all(blocks, ("x", "zl"), 0, 0, tiled=True)
    weight_grad, gain_grad = call(
        finish_kernel, "finish", "v", (blocks,),
        (shape((27, 12, 2 * C), f32), shape((1, C), f32)), [pltpu.VMEM((672, 128), f32)] * 2,
    )
    return (
        decoded[None, :, None],
        latent_grad[None, :, None],
        weight_grad.reshape(3, 3, 3, 12, 2 * C),
        gain_grad.reshape(C),
    )


def solution(mesh):
    names = ("x", "zh", "zl", "yh", "yl", "core")
    axes = Mesh(mesh.devices.reshape(NX, NH, NL, 2, 2, NCORE), names)
    dp, clip = ("yh", "yl", "core"), ("x", "zh", "zl")
    data = P(dp, None, clip, None, None, None)
    kernel = P(None, None, None, dp, None)
    return jax.shard_map(
        on_device,
        mesh=axes,
        in_specs=(data, data, kernel, P(), P(dp, None)),
        out_specs=(data, data, kernel, P()),
        check_vma=False,
    )
```
